32 devices in a mesh: ctx: 16 (over z, y, x), tp: 2 (over core).
Axes of the slice: x: 2, y: 2, z: 4, core: 2. Of those that a mesh axis runs over, the one named last changes fastest.
Arguments:
- hyena_in: bfloat16 [4096, 3, 4096], P('ctx', None, 'tp'), may hold values from -6 to 6
- filters: float32 [128, 4096], P(None, 'tp'), may hold values from -0.5 to 0.5
- attn_in: bfloat16 [4096, 3, 4096], P('ctx', None, 'tp'), may hold values from -18.5 to 18.5
- out_weight: bfloat16 [4096, 4096], P('tp', 'ctx'), may hold values from -0.125 to 0.125
- attn_weight: bfloat16 [4096, 4096], P('tp', 'ctx'), may hold values from -0.125 to 0.125
Outputs:
- block_out: bfloat16 [4096, 4096], P('ctx', 'tp')
- attn_block: bfloat16 [4096, 4096], P('ctx', 'tp')
The draws below stay inside these ranges and needn't reach their ends.
All inputs are finite; a program needn't handle non-finite values.
Results may differ from the reference program's by a relative error of at most 0.014.
Values may be sent and summed in bfloat16 or wider, within the bound.
No kernel may reach another device: no remote copies, remote signals or barrier semaphores. Data moves between devices by JAX's collectives and lax.ppermute only.
A program may use at most 128 MiB of HBM per device.

```python
import math
import jax
import jax.numpy as jnp
from jax import lax

D = 4096
HEADS = 32
HEAD_DIM = 128
TAPS = 128
WINDOW = 2048
CHANNELS = 4096
TOKENS = 4096
N_TP = 2


def draw_attn_in(key, part):
    key_query, key_keys, key_values = jax.random.split(jax.random.fold_in(key, 7), 3)
    shape = (TOKENS, CHANNELS)
    queries = jnp.clip(jax.random.normal(key_query, shape, jnp.float32), -4.0, 4.0)
    keys_drawn = 3.0 * jnp.clip(jax.random.normal(key_keys, shape, jnp.float32), -4.0, 4.0)
    values = jnp.clip(jax.random.normal(key_values, shape, jnp.float32), -4.0, 4.0)
    return jnp.stack([queries, keys_drawn, values], 1).astype(jnp.bfloat16)


def with_spikes(values, rng, source, target, parts, factor):
    def block_of(dim):
        return (jnp.arange(values.shape[dim]) // (values.shape[dim] // parts)).reshape((-1,) + (1,) * (values.ndim - 1 - dim))

    first = jax.random.permutation(rng, parts)[block_of(target)]
    second = (block_of(target) + parts // 2) % parts
    return jnp.where((block_of(source) == first) | (block_of(source) == second), factor * values, values)


def shard_levels(stream_key, dims, cuts, smallest, largest):
    factor_of, own = 1.0, jax.random.fold_in(stream_key, 6)
    for dim, blocks in cuts:
        draws = jnp.exp(jax.random.uniform(jax.random.fold_in(own, dim), (blocks,), jnp.float32, smallest / len(cuts), largest / len(cuts)))
        factor_of = factor_of * jnp.repeat(draws, dims[dim] // blocks).reshape([-1 if axis == dim else 1 for axis in range(len(dims))])
    return factor_of


def normal_values(key, dims, spread, most, cuts=(), held_as=jnp.bfloat16):
    factor_of = shard_levels(key, dims, cuts, -0.22, 0.18) if cuts else 1.0
    entries = jax.random.normal(key, dims, jnp.float32) * spread * factor_of
    return jnp.minimum(jnp.maximum(entries, -most), most).astype(held_as)


def heavy_noise(rng, dims, spread, bound, cuts, heavy, held_as=jnp.bfloat16):
    values = spread * jax.random.normal(rng, dims, jnp.float32)
    if cuts:
        values = values * shard_levels(rng, dims, cuts, -0.22, 0.18)
    return jnp.clip(with_spikes(values, jax.random.fold_in(rng, 3), *heavy), -bound, bound).astype(held_as)


def setup_inputs(seed: int = 0) -> dict:
    splits = jax.random.split(jax.random.key(seed), 6)
    return {
        "hyena_in": normal_values(splits[0], (TOKENS, 3, CHANNELS), 1.0, 6.0, ((0, 16), (2, 2))),
        "filters": normal_values(splits[1], (TAPS, CHANNELS), TAPS ** -0.5, 0.5, ((1, 2),), jnp.float32),
        "attn_in": draw_attn_in(jax.random.fold_in(splits[5], 71), 0),
        "out_weight": heavy_noise(splits[3], (CHANNELS, D), CHANNELS ** -0.5, 0.125, ((0, 2), (1, 16)), (0, 1, 16, 2.0)),
        "attn_weight": heavy_noise(splits[4], (CHANNELS, D), CHANNELS ** -0.5, 0.125, ((0, 2), (1, 16)), (0, 1, 16, 2.0)),
    }


def depthwise(padded, filters):
    taps = filters.shape[0]
    length = padded.shape[0] - taps + 1

    def add_tap(index, total):
        window_rows = lax.dynamic_slice_in_dim(padded, (taps - 1 - index).astype(jnp.int32), length, 0)
        return total + filters[index][None, :] * window_rows
    return lax.fori_loop(0, taps, add_tap, jnp.zeros((length, padded.shape[1]), jnp.float32))

def head_attention(queries, keys_all, values_all, first_query, first_key):
    scores = lax.dot_general(queries, keys_all, (((1,), (1,)), ((), ())), preferred_element_type=jnp.float32)
    scores = scores * (1.0 / math.sqrt(HEAD_DIM))
    query_pos = first_query + lax.iota(jnp.int32, queries.shape[0])
    key_pos = first_key + lax.iota(jnp.int32, keys_all.shape[0])
    valid = (key_pos[None, :] <= query_pos[:, None]) & (key_pos[None, :] > query_pos[:, None] - WINDOW) & (key_pos[None, :] >= 0)
    scores = jnp.where(valid, scores, -jnp.inf)
    top = lax.optimization_barrier(jnp.max(scores, axis=1, keepdims=True))
    weights = jnp.exp(scores - top)
    total = lax.optimization_barrier(jnp.sum(weights, axis=1, keepdims=True))
    probs = weights.astype(jnp.bfloat16)
    return jnp.dot(probs, values_all, preferred_element_type=jnp.float32) / total

def split_heads(array):
    return array.reshape(array.shape[0], HEADS, HEAD_DIM).transpose(1, 0, 2)

def project_groups(acts, weight):
    width = CHANNELS // N_TP
    summed = jnp.zeros((TOKENS, D), jnp.float32)
    for group in range(N_TP):
        term = jnp.dot(acts[:, group * width:(group + 1) * width], weight[group * width:(group + 1) * width], preferred_element_type=jnp.float32).astype(jnp.bfloat16)
        term = lax.optimization_barrier(term)
        summed = summed + term.astype(jnp.float32)
    return summed.astype(jnp.bfloat16)

def reference(hyena_in, filters, attn_in, out_weight, attn_weight):
    product = (hyena_in[:, 0].astype(jnp.float32) * hyena_in[:, 2].astype(jnp.float32)).astype(jnp.bfloat16)
    padded = jnp.concatenate([jnp.zeros((TAPS - 1, CHANNELS), jnp.float32), product.astype(jnp.float32)], 0)
    filtered = depthwise(padded, filters)
    hyena_act = (hyena_in[:, 1].astype(jnp.float32) * filtered).astype(jnp.bfloat16)
    block = math.gcd(TOKENS, 512)
    padding = jnp.zeros((WINDOW, CHANNELS), jnp.bfloat16)
    query_heads = split_heads(attn_in[:, 0])
    key_heads = split_heads(jnp.concatenate([padding, attn_in[:, 1]], 0))
    value_heads = split_heads(jnp.concatenate([padding, attn_in[:, 2]], 0))
    starts = jnp.arange(TOKENS // block, dtype=jnp.int32) * block

    def one_head(operands):
        query_one, key_one, value_one = operands

        def one_block(start):
            query_block = lax.dynamic_slice_in_dim(query_one, start, block, 0)
            key_block = lax.dynamic_slice_in_dim(key_one, start, block + WINDOW, 0)
            value_block = lax.dynamic_slice_in_dim(value_one, start, block + WINDOW, 0)
            return head_attention(query_block, key_block, value_block, start, start - WINDOW)
        return lax.map(one_block, starts).reshape(TOKENS, HEAD_DIM)
    attended = lax.map(one_head, (query_heads, key_heads, value_heads))
    attended = attended.transpose(1, 0, 2).reshape(TOKENS, CHANNELS).astype(jnp.bfloat16)
    return (project_groups(hyena_act, out_weight), project_groups(attended, attn_weight))
```

```python
import functools
import math

import jax
import jax.numpy as jnp
import ml_dtypes
import numpy as np
from jax import lax
from jax.experimental import pallas as pl
from jax.experimental.pallas import tpu as pltpu
from jax.sharding import PartitionSpec as P

HEAD_DIM = 128
WINDOW = 2048
PLANE = 4
MASKED = -1e30
VMEM = 56 * 1024 * 1024


def split_bf16(array):
    high = array.astype(jnp.bfloat16)
    return high, (array - high.astype(jnp.float32)).astype(jnp.bfloat16)


def mm(a, b):
    return jnp.dot(a, b, preferred_element_type=jnp.float32)


def dft_matrices(taps):
    size = 2 * taps
    n = np.arange(size)
    k = np.arange(taps)
    angle = 2 * np.pi * ((k[:, None] * n[None, :]) % size) / size
    cosine, sine = np.cos(angle), np.sin(angle)
    forward = np.concatenate([cosine, -sine], 0)
    forward[taps] = (-1.0) ** n
    weight = np.full(taps, 2.0 / size)
    weight[0] = 1.0 / size
    inverse = np.concatenate([cosine * weight[:, None], -sine * weight[:, None]], 0)
    inverse[taps] = (-1.0) ** n / size
    inverse = inverse.T[taps:]

    def halves(array):
        array = array.astype(np.float32)
        high = array.astype(ml_dtypes.bfloat16)
        return high, (array - high.astype(np.float32)).astype(ml_dtypes.bfloat16)

    return [jnp.asarray(m) for m in halves(forward) + halves(inverse)]


def fir_kernel(rim, product, gate, filters, f_hi, f_lo, g_hi, g_lo, out):
    taps = filters.shape[0]
    rows = product.shape[0]
    h_hi, h_lo = split_bf16(filters[...])
    spectrum = (
        mm(f_hi[:, :taps], h_hi) + mm(f_hi[:, :taps], h_lo) + mm(f_lo[:, :taps], h_hi)
    )
    first = lax.broadcasted_iota(jnp.int32, (taps, spectrum.shape[1]), 0) == 0
    h_re, h_im = spectrum[:taps], spectrum[taps:]
    h_re2 = jnp.where(first, h_im, h_re)
    h_im = jnp.where(first, 0.0, h_im)
    for start in range(0, rows, taps):
        before = rim[...] if start == 0 else product[start - taps : start]
        x = jnp.concatenate([before, product[start : start + taps]], 0)
        xs = mm(f_hi[...], x) + mm(f_lo[...], x)
        x_re, x_im = xs[:taps], xs[taps:]
        y = jnp.concatenate([x_re * h_re - x_im * h_im, x_re * h_im + x_im * h_re2], 0)
        y_hi, y_lo = split_bf16(y)
        filtered = mm(g_hi[...], y_hi) + mm(g_hi[...], y_lo) + mm(g_lo[...], y_hi)
        span = slice(start, start + taps)
        out[span] = (gate[span].astype(jnp.float32) * filtered).astype(out.dtype)


def fir(rim, product, gate, filters):
    taps, width = filters.shape
    rows = product.shape[0]
    tile = min(512, width)
    mats = dft_matrices(taps)
    column = lambda n: pl.BlockSpec((n, tile), lambda i: (0, i))
    return pl.pallas_call(
        fir_kernel,
        grid=(width // tile,),
        in_specs=[column(taps), column(rows), column(rows), column(taps)]
        + [pl.BlockSpec(m.shape, lambda i: (0, 0)) for m in mats],
        out_specs=column(rows),
        out_shape=jax.ShapeDtypeStruct((rows, width), jnp.bfloat16),
        compiler_params=pltpu.CompilerParams(vmem_limit_bytes=VMEM),
        cost_estimate=pl.CostEstimate(
            flops=2 * width * (10 * rows * taps + 6 * taps * taps),
            bytes_accessed=8 * rows * width,
            transcendentals=0,
        ),
    )(rim, product, gate, filters, *mats)


def attend_kernel(kind, first, last, info, q_ref, k_ref, v_ref, *refs):
    refs = list(refs)
    if not first:
        acc_in, stat_in = refs.pop(0), refs.pop(0)
    if last:
        (out,) = refs
    else:
        acc_out, stat_out = refs
    plane, rows = k_ref.shape[0], k_ref.shape[2]
    me = info[0]
    factor = math.log2(math.e) / math.sqrt(HEAD_DIM)
    lane = lax.broadcasted_iota(jnp.int32, (rows, HEAD_DIM), 1)

    def write(top, total, acc):
        if last:
            out[0] = (acc / total).astype(out.dtype)
        else:
            acc_out[0] = acc
            stat_out[0] = jnp.where(lane < HEAD_DIM // 2, top, total)

    def previous():
        stat = stat_in[0]
        half = HEAD_DIM // 2
        return stat[:, 0:1], stat[:, half : half + 1], acc_in[0]

    def attend(blocks, diagonal):
        q = q_ref[0]
        scores = []
        for j in blocks:
            s = lax.dot_general(
                q, k_ref[me ^ j, 0], (((1,), (1,)), ((), ())), preferred_element_type=jnp.float32
            ) * factor
            if j == diagonal:
                row = lax.broadcasted_iota(jnp.int32, s.shape, 0)
                col = lax.broadcasted_iota(jnp.int32, s.shape, 1)
                s = jnp.where(col <= row if kind == "causal" else col > row, s, MASKED)
            scores.append(s)
        top = functools.reduce(jnp.maximum, scores).max(axis=1, keepdims=True)
        if not first:
            old_top, old_total, old_acc = previous()
            top = jnp.maximum(top, old_top)
        acc, sums = None, None
        for j, s in zip(blocks, scores):
            w = jnp.exp2(s - top)
            sums = w if sums is None else sums + w
            term = mm(w.astype(jnp.bfloat16), v_ref[me ^ j, 0])
            acc = term if acc is None else acc + term
        total = sums.sum(axis=1, keepdims=True)
        if not first:
            shrink = jnp.exp2(old_top - top)
            total = total + shrink * old_total
            acc = acc + shrink * old_acc
        write(top, total, acc)

    def run():
        if kind == "full":
            attend(list(range(plane)), None)
            return
        here = pl.program_id(1)
        for i in range(plane):

            @pl.when(here == i)
            def _(i=i):
                attend(list(range(i + 1)) if kind == "causal" else list(range(i, plane)), i)

    if first:
        run()
    else:

        @pl.when(info[1] > 0)
        def _():
            run()

        @pl.when(info[1] == 0)
        def _():
            write(*previous())


def attend(kind, first, last, info, queries, pairs, carry):
    plane, rows, width = queries.shape
    heads = width // HEAD_DIM
    mine = pl.BlockSpec((1, rows, HEAD_DIM), lambda h, i, info: (info[0] ^ i, 0, h))
    keys = pl.BlockSpec((plane, 1, rows, HEAD_DIM), lambda h, i, info: (0, 0, 0, h))
    values = pl.BlockSpec((plane, 1, rows, HEAD_DIM), lambda h, i, info: (0, 1, 0, h))
    if last:
        out_specs, out_shape = mine, jax.ShapeDtypeStruct(queries.shape, jnp.bfloat16)
    else:
        out_specs = (mine, mine)
        out_shape = (jax.ShapeDtypeStruct(queries.shape, jnp.float32),) * 2
    scores = heads * (plane * rows) ** 2 // (1 if kind == "full" else 2)
    return pl.pallas_call(
        functools.partial(attend_kernel, kind, first, last),
        grid_spec=pltpu.PrefetchScalarGridSpec(
            num_scalar_prefetch=1,
            grid=(heads, plane),
            in_specs=[mine, keys, values] + [mine] * len(carry),
            out_specs=out_specs,
        ),
        out_shape=out_shape,
        compiler_params=pltpu.CompilerParams(vmem_limit_bytes=VMEM),
        cost_estimate=pl.CostEstimate(
            flops=4 * scores * HEAD_DIM, bytes_accessed=12 * queries.size, transcendentals=scores
        ),
    )(info, queries, pairs, pairs, *carry)


def project_kernel(levels, splits, info, *refs):
    parts, weights, out = refs[:splits], refs[splits:-1], refs[-1]
    level = info[0]
    depth = parts[0].shape[2]
    for index, w in enumerate(weights):
        target = level + (index - (levels - 1))

        @pl.when((target >= 0) & (target < levels))
        def _(w=w, target=target):
            total = None
            for s, part in enumerate(parts):
                term = mm(part[0], w[s * depth : (s + 1) * depth])
                total = term if total is None else total + term
            out[target, 0] = total.astype(out.dtype)


def project(levels, info, parts, weights):
    plane, rows, depth = parts[0].shape
    columns = weights[0].shape[1]

    def part_spec(s):
        return pl.BlockSpec((1, rows, depth), lambda r, info: (r ^ s, 0, 0))

    return pl.pallas_call(
        functools.partial(project_kernel, levels, len(parts)),
        grid_spec=pltpu.PrefetchScalarGridSpec(
            num_scalar_prefetch=1,
            grid=(plane,),
            in_specs=[part_spec(s) for s in range(len(parts))]
            + [pl.BlockSpec(w.shape, lambda r, info: (0, 0)) for w in weights],
            out_specs=pl.BlockSpec((levels, 1, rows, columns), lambda r, info: (0, r, 0, 0)),
        ),
        out_shape=jax.ShapeDtypeStruct((levels, plane, rows, columns), jnp.bfloat16),
        compiler_params=pltpu.CompilerParams(vmem_limit_bytes=VMEM),
        cost_estimate=pl.CostEstimate(
            flops=2 * plane * rows * depth * len(parts) * columns * levels,
            bytes_accessed=16 * 1024 * 1024,
            transcendentals=0,
        ),
    )(info, *parts, *weights)


def per_device(hyena_in, filters, attn_in, out_weight, attn_weight):
    rows, _, width = hyena_in.shape
    taps = filters.shape[0]
    n_ctx, n_tp = lax.axis_size("ctx"), lax.axis_size("tp")
    levels = n_ctx // PLANE
    device_index = lax.axis_index("ctx")
    group = lax.axis_index("tp")
    me, level = device_index % PLANE, device_index // PLANE
    chunk = width // PLANE

    def swap(block, relative):
        return lax.ppermute(block, "ctx", [(i, i ^ relative) for i in range(n_ctx)])

    def climb(block, direction, step):
        if direction > 0:
            sources = range((step - 1) * PLANE, n_ctx - PLANE)
        else:
            sources = range(PLANE, n_ctx - (step - 1) * PLANE)
        return lax.ppermute(block, "ctx", [(i, i + direction * PLANE) for i in sources])

    def by_relative(build):
        return [build(me ^ s) for s in range(PLANE)]

    def piece(first, count, index):
        block = lax.dynamic_slice(attn_in, (0, first, index * chunk), (rows, count, chunk))
        return block.transpose(1, 0, 2)

    pair_pieces = by_relative(lambda index: piece(1, 2, index))
    query_pieces = by_relative(lambda index: piece(0, 1, index)[0])
    pairs = jnp.stack([pair_pieces[0]] + [swap(pair_pieces[s], s) for s in range(1, PLANE)])
    queries = jnp.stack([query_pieces[0]] + [swap(query_pieces[s], s) for s in range(1, PLANE)])

    attn_rows = attn_weight.reshape(PLANE, chunk, -1)
    attn_weight = jnp.concatenate(
        by_relative(lambda index: lax.dynamic_index_in_dim(attn_rows, index, 0, False)), 0
    )

    def along_levels(weight):
        up, down = [weight], [weight]
        for step in range(1, levels):
            up.append(climb(up[-1], 1, step))
            down.append(climb(down[-1], -1, step))
        return up[:0:-1] + down

    product = (hyena_in[:, 0].astype(jnp.float32) * hyena_in[:, 2].astype(jnp.float32)).astype(
        jnp.bfloat16
    )
    rim = lax.ppermute(
        product[rows - taps :], "ctx", [(i, i + 1) for i in range(n_ctx - 1)]
    )
    hyena_act = fir(rim, product, hyena_in[:, 1], filters)

    def across_plane(block):
        one, two = swap(block, 1), swap(block, 2)
        half = block.shape[0] // 2
        three = jnp.concatenate([swap(one[:half], 2), swap(two[half:], 1)], 0)
        return [block, one, two, three]

    hyena_rows = jnp.stack(across_plane(hyena_act))

    back = WINDOW // (PLANE * rows)
    carry = ()
    for distance in range(back + 1):
        if distance:
            pairs = climb(pairs, 1, 1)
        kind = "causal" if distance == 0 else "full" if distance < back else "anti"
        info = jnp.stack([me, (level >= distance).astype(jnp.int32)]).astype(jnp.int32)
        carry = attend(kind, distance == 0, distance == back, info, queries, pairs, carry)
    attended = across_plane(carry)

    level_info = jnp.stack([level]).astype(jnp.int32)
    share = levels // n_tp

    def finish(parts, weight):
        partial = project(levels, level_info, parts, along_levels(weight))
        partial = partial.reshape((n_tp, share) + partial.shape[1:])
        total = lax.dynamic_index_in_dim(partial, group, 0, False).astype(jnp.float32)
        for shift in range(1, n_tp):
            sent = lax.dynamic_index_in_dim(partial, (group + shift) % n_tp, 0, False)
            got = lax.ppermute(sent, "tp", [(i, (i + shift) % n_tp) for i in range(n_tp)])
            total = total + got.astype(jnp.float32)
        total = total.astype(jnp.bfloat16)
        ours = [total[:, 0]] + [swap(total[:, s], s) for s in range(1, PLANE)]
        natural = [
            lax.select_n(me, *[ours[t ^ j] for t in range(PLANE)]) for j in range(PLANE)
        ]
        return jnp.stack(natural, 1).transpose(2, 0, 1, 3).reshape(rows, -1)

    return (finish([hyena_rows], out_weight), finish(attended, attn_weight))


def solution(mesh):
    in_specs = (
        P("ctx", None, "tp"),
        P(None, "tp"),
        P("ctx", None, "tp"),
        P("tp", "ctx"),
        P("tp", "ctx"),
    )
    out_specs = (P("ctx", "tp"), P("ctx", "tp"))
    return jax.shard_map(
        per_device, mesh=mesh, in_specs=in_specs, out_specs=out_specs, check_vma=False
    )
```

```python
import functools
import math

import jax
import jax.numpy as jnp
import ml_dtypes
import numpy as np
from jax import lax
from jax.experimental import pallas as pl
from jax.experimental.pallas import tpu as pltpu
from jax.sharding import PartitionSpec as P

HEAD_DIM = 128
WINDOW = 2048
PLANE = 4
MASKED = -1e30
VMEM = 56 * 1024 * 1024


def split_bf16(array):
    high = array.astype(jnp.bfloat16)
    return high, (array - high.astype(jnp.float32)).astype(jnp.bfloat16)


def mm(a, b):
    return jnp.dot(a, b, preferred_element_type=jnp.float32)


def dft_matrices(taps):
    size = 2 * taps
    n = np.arange(size)
    k = np.arange(taps)
    angle = 2 * np.pi * ((k[:, None] * n[None, :]) % size) / size
    cosine, sine = np.cos(angle), np.sin(angle)
    forward = np.concatenate([cosine, -sine], 0)
    forward[taps] = (-1.0) ** n
    weight = np.full(taps, 2.0 / size)
    weight[0] = 1.0 / size
    inverse = np.concatenate([cosine * weight[:, None], -sine * weight[:, None]], 0)
    inverse[taps] = (-1.0) ** n / size
    inverse = inverse.T[taps:]

    def halves(array):
        array = array.astype(np.float32)
        high = array.astype(ml_dtypes.bfloat16)
        return high, (array - high.astype(np.float32)).astype(ml_dtypes.bfloat16)

    return [jnp.asarray(m) for m in halves(forward) + halves(inverse)]


def fir_kernel(rim, product, gate, filters, f_hi, f_lo, g_hi, g_lo, out):
    taps = filters.shape[0]
    rows = product.shape[0]
    h_hi, h_lo = split_bf16(filters[...])
    spectrum = (
        mm(f_hi[:, :taps], h_hi) + mm(f_hi[:, :taps], h_lo) + mm(f_lo[:, :taps], h_hi)
    )
    first = lax.broadcasted_iota(jnp.int32, (taps, spectrum.shape[1]), 0) == 0
    h_re, h_im = spectrum[:taps], spectrum[taps:]
    h_re2 = jnp.where(first, h_im, h_re)
    h_im = jnp.where(first, 0.0, h_im)
    for start in range(0, rows, taps):
        before = rim[...] if start == 0 else product[start - taps : start]
        x = jnp.concatenate([before, product[start : start + taps]], 0)
        xs = mm(f_hi[...], x) + mm(f_lo[...], x)
        x_re, x_im = xs[:taps], xs[taps:]
        y = jnp.concatenate([x_re * h_re - x_im * h_im, x_re * h_im + x_im * h_re2], 0)
        y_hi, y_lo = split_bf16(y)
        filtered = mm(g_hi[...], y_hi) + mm(g_hi[...], y_lo) + mm(g_lo[...], y_hi)
        span = slice(start, start + taps)
        out[span] = (gate[span].astype(jnp.float32) * filtered).astype(out.dtype)


def fir(rim, product, gate, filters):
    taps, width = filters.shape
    rows = product.shape[0]
    tile = min(512, width)
    mats = dft_matrices(taps)
    column = lambda n: pl.BlockSpec((n, tile), lambda i: (0, i))
    return pl.pallas_call(
        fir_kernel,
        grid=(width // tile,),
        in_specs=[column(taps), column(rows), column(rows), column(taps)]
        + [pl.BlockSpec(m.shape, lambda i: (0, 0)) for m in mats],
        out_specs=column(rows),
        out_shape=jax.ShapeDtypeStruct((rows, width), jnp.bfloat16),
        compiler_params=pltpu.CompilerParams(vmem_limit_bytes=VMEM),
        cost_estimate=pl.CostEstimate(
            flops=2 * width * (10 * rows * taps + 6 * taps * taps),
            bytes_accessed=8 * rows * width,
            transcendentals=0,
        ),
    )(rim, product, gate, filters, *mats)


def attend_kernel(kind, first, last, info, q_ref, k_ref, v_ref, *refs):
    refs = list(refs)
    if not first:
        acc_in, stat_in = refs.pop(0), refs.pop(0)
    out, stat_out = refs
    plane, rows = k_ref.shape[0], k_ref.shape[2]
    me = info[0]
    factor = math.log2(math.e) / math.sqrt(HEAD_DIM)
    half = HEAD_DIM // 2

    def write(i, top, total, acc):
        if last:
            out[me ^ i] = (acc * (1.0 / total)).astype(out.dtype)
            level = jnp.broadcast_to(top + jnp.log2(total), (rows, HEAD_DIM))
            stat_out[0, me ^ i] = level.T[0:8]
        else:
            out[me ^ i] = acc
            lane = lax.broadcasted_iota(jnp.int32, (rows, HEAD_DIM), 1)
            stat_out[me ^ i] = jnp.where(lane < half, top, total)

    def previous(i):
        stat = stat_in[me ^ i]
        return stat[:, 0:1], stat[:, half : half + 1], acc_in[me ^ i]

    def attend(i):
        blocks = range(plane)
        if kind != "full":
            blocks = range(i + 1) if kind == "causal" else range(i, plane)
        q = q_ref[me ^ i]
        scores = []
        for j in blocks:
            s = lax.dot_general(
                q, k_ref[me ^ j, 0], (((1,), (1,)), ((), ())), preferred_element_type=jnp.float32
            ) * factor
            if j == i and kind != "full":
                row = lax.broadcasted_iota(jnp.int32, s.shape, 0)
                col = lax.broadcasted_iota(jnp.int32, s.shape, 1)
                s = jnp.where(col <= row if kind == "causal" else col > row, s, MASKED)
            scores.append(s)
        top = functools.reduce(jnp.maximum, scores).max(axis=1, keepdims=True)
        if not first:
            old_top, old_total, old_acc = previous(i)
            top = jnp.maximum(top, old_top)
        acc, sums = None, None
        for j, s in zip(blocks, scores):
            w = jnp.exp2(s - top)
            sums = w if sums is None else sums + w
            term = mm(w.astype(jnp.bfloat16), v_ref[me ^ j, 0])
            acc = term if acc is None else acc + term
        total = sums.sum(axis=1, keepdims=True)
        if not first:
            shrink = jnp.exp2(old_top - top)
            total = total + shrink * old_total
            acc = acc + shrink * old_acc
        write(i, top, total, acc)

    def run():
        for i in range(plane):
            attend(i)

    if first:
        run()
    else:

        @pl.when(info[1] > 0)
        def _():
            run()

        @pl.when(info[1] == 0)
        def _():
            for i in range(plane):
                write(i, *previous(i))


def attend(kind, last, info, queries, pairs, carry=(), dtype=jnp.float32):
    plane, rows, width = queries.shape
    heads = width // HEAD_DIM
    mine = pl.BlockSpec((plane, rows, HEAD_DIM), lambda h, info: (0, 0, h))
    keys = pl.BlockSpec((plane, 1, rows, HEAD_DIM), lambda h, info: (0, 0, 0, h))
    values = pl.BlockSpec((plane, 1, rows, HEAD_DIM), lambda h, info: (0, 1, 0, h))
    state = jax.ShapeDtypeStruct(queries.shape, jnp.float32)
    if last:
        out_specs = (mine, pl.BlockSpec((1, plane, 8, rows), lambda h, info: (h, 0, 0, 0)))
        out_shape = (
            jax.ShapeDtypeStruct(queries.shape, dtype),
            jax.ShapeDtypeStruct((heads, plane, 8, rows), jnp.float32),
        )
    else:
        out_specs, out_shape = (mine, mine), (state, state)
    scores = heads * (plane * rows) ** 2 // (1 if kind == "full" else 2)
    return pl.pallas_call(
        functools.partial(attend_kernel, kind, not carry, last),
        grid_spec=pltpu.PrefetchScalarGridSpec(
            num_scalar_prefetch=1,
            grid=(heads,),
            in_specs=[mine, keys, values] + [mine] * len(carry),
            out_specs=out_specs,
        ),
        out_shape=out_shape,
        compiler_params=pltpu.CompilerParams(vmem_limit_bytes=VMEM),
        cost_estimate=pl.CostEstimate(
            flops=4 * scores * HEAD_DIM, bytes_accessed=12 * queries.size, transcendentals=scores
        ),
    )(info, queries, pairs, pairs, *carry)


def merge_kernel(info, one_ref, level_one, two_ref, level_two, out):
    rows = one_ref.shape[1]
    for h in range(one_ref.shape[2] // HEAD_DIM):
        span = slice(h * HEAD_DIM, (h + 1) * HEAD_DIM)
        one, two = level_one[h, 0, 0:1], level_two[h, 0, 0:1]
        two = jnp.where(info[0] > 0, two, MASKED)
        top = jnp.maximum(one, two)
        one, two = jnp.exp2(one - top), jnp.exp2(two - top)
        share = jnp.broadcast_to(two * (1.0 / (one + two)), (HEAD_DIM, rows)).T
        first, second = one_ref[0, :, span], two_ref[0, :, span].astype(jnp.float32)
        out[0, :, span] = (first + share * (second - first)).astype(out.dtype)


def merge(info, one, level_one, two, level_two):
    plane, rows, width = one.shape
    block = pl.BlockSpec((1, rows, width), lambda i, info: (i, 0, 0))
    level = pl.BlockSpec((level_one.shape[0], 1, 8, rows), lambda i, info: (0, i, 0, 0))
    return pl.pallas_call(
        merge_kernel,
        grid_spec=pltpu.PrefetchScalarGridSpec(
            num_scalar_prefetch=1,
            grid=(plane,),
            in_specs=[block, level, block, level],
            out_specs=block,
        ),
        out_shape=jax.ShapeDtypeStruct(one.shape, jnp.bfloat16),
        compiler_params=pltpu.CompilerParams(vmem_limit_bytes=VMEM),
        cost_estimate=pl.CostEstimate(
            flops=4 * one.size, bytes_accessed=8 * one.size, transcendentals=0
        ),
    )(info, one, level_one, two, level_two)


def project_kernel(levels, n_tp, splits, by_rows, info, *refs):
    parts, weights = refs[:splits], refs[splits:-4]
    mine, others, a, acc = refs[-4:]
    level, group, step = info[0], info[1], pl.program_id(0)
    plane = mine.shape[0]
    rows = a.shape[0] // plane
    share = levels // n_tp
    if by_rows:
        for r, part in enumerate(parts):
            a[r * rows : (r + 1) * rows] = part[...]
    else:
        for s, part in enumerate(parts):

            @pl.when(step == s)
            def _(s=s, part=part):
                for r in range(plane):
                    a[r * rows : (r + 1) * rows] = part[r ^ s]

    @pl.when(step == 0)
    def _():
        acc[...] = jnp.zeros_like(acc)

    for index, w in enumerate(weights):
        target = level + (index - (levels - 1))

        @pl.when((target >= 0) & (target < levels))
        def _(w=w, target=target):
            acc[target] += mm(a[...], w[...])

    @pl.when(step == pl.num_programs(0) - 1)
    def _():
        for t in range(levels):
            ahead = (t // share + n_tp - group) % n_tp

            @pl.when(ahead == 0)
            def _(t=t):
                for r in range(plane):
                    mine[r, t % share] = acc[t, r * rows : (r + 1) * rows].astype(mine.dtype)

            @pl.when(ahead > 0)
            def _(t=t, ahead=ahead):
                for r in range(plane):
                    others[ahead - 1, r, t % share] = acc[t, r * rows : (r + 1) * rows].astype(
                        others.dtype
                    )


def project(levels, n_tp, info, parts, weights):
    by_rows = parts[0].ndim == 2
    weights = [w if isinstance(w, tuple) else (w[None], 0) for w in weights]
    width, columns = weights[0][0].shape[1:]
    rows = parts[0].shape[-2]
    depth = width // PLANE
    share = levels // n_tp
    if by_rows:
        part_spec = pl.BlockSpec((rows, depth), lambda k, info: (0, k))
    else:
        part_spec = pl.BlockSpec((PLANE, rows, depth), lambda k, info: (0, 0, 0))
    block = (PLANE, share, rows, columns)
    return pl.pallas_call(
        functools.partial(project_kernel, levels, n_tp, len(parts), by_rows),
        grid_spec=pltpu.PrefetchScalarGridSpec(
            num_scalar_prefetch=1,
            grid=(PLANE,),
            in_specs=[part_spec] * len(parts)
            + [
                pl.BlockSpec((pl.squeezed, depth, columns), lambda k, info, i=i: (i, k, 0))
                for _, i in weights
            ],
            out_specs=(
                pl.BlockSpec(block, lambda k, info: (0,) * 4),
                pl.BlockSpec((n_tp - 1,) + block, lambda k, info: (0,) * 5),
            ),
            scratch_shapes=[
                pltpu.VMEM((PLANE * rows, depth), jnp.bfloat16),
                pltpu.VMEM((levels, PLANE * rows, columns), jnp.float32),
            ],
        ),
        out_shape=(
            jax.ShapeDtypeStruct(block, jnp.bfloat16),
            jax.ShapeDtypeStruct((n_tp - 1,) + block, jnp.bfloat16),
        ),
        compiler_params=pltpu.CompilerParams(vmem_limit_bytes=VMEM),
        cost_estimate=pl.CostEstimate(
            flops=2 * PLANE * rows * width * columns * levels,
            bytes_accessed=16 * 1024 * 1024,
            transcendentals=0,
        ),
    )(info, *parts, *[w for w, _ in weights])


def assemble_kernel(info, *refs):
    pieces, out = refs[:-1], refs[-1]
    share, rows, columns = pieces[0].shape
    for s, piece in enumerate(pieces):
        for t in range(share):
            start = pl.multiple_of((t * PLANE + (info[0] ^ s)) * columns, columns)
            out[:, pl.ds(start, columns)] = piece[t]


def assemble(info, pieces):
    share, rows, columns = pieces[0].shape
    if columns % 128:
        natural = [
            lax.select_n(info[0], *[pieces[t ^ j] for t in range(PLANE)]) for j in range(PLANE)
        ]
        return jnp.stack(natural, 1).transpose(2, 0, 1, 3).reshape(rows, -1)
    return pl.pallas_call(
        assemble_kernel,
        grid_spec=pltpu.PrefetchScalarGridSpec(
            num_scalar_prefetch=1,
            grid=(1,),
            in_specs=[pl.BlockSpec(p.shape, lambda i, info: (0, 0, 0)) for p in pieces],
            out_specs=pl.BlockSpec((rows, share * PLANE * columns), lambda i, info: (0, 0)),
        ),
        out_shape=jax.ShapeDtypeStruct((rows, share * PLANE * columns), jnp.bfloat16),
        compiler_params=pltpu.CompilerParams(vmem_limit_bytes=VMEM),
    )(info, *pieces)


def per_device(hyena_in, filters, attn_in, out_weight, attn_weight):
    rows, _, width = hyena_in.shape
    taps = filters.shape[0]
    n_ctx, n_tp = lax.axis_size("ctx"), lax.axis_size("tp")
    levels = n_ctx // PLANE
    device_index = lax.axis_index("ctx")
    group = lax.axis_index("tp")
    me, level = device_index % PLANE, device_index // PLANE
    chunk = width // PLANE
    assert WINDOW == 2 * PLANE * rows and levels > 2 and levels % n_tp == 0

    def flags(*values):
        return jnp.stack([jnp.asarray(v).astype(jnp.int32) for v in values])

    def after(value, *others):
        return lax.optimization_barrier((value, *others))[0]

    def swap(block, relative):
        return lax.ppermute(block, "ctx", [(i, i ^ relative) for i in range(n_ctx)])

    def move(block, direction, first, last):
        sources = range(first * PLANE, (last + 1) * PLANE)
        return lax.ppermute(block, "ctx", [(i, i + direction * PLANE) for i in sources])

    def climb(block, direction, step=1):
        if direction > 0:
            return move(block, 1, step - 1, levels - 2)
        return move(block, -1, 1, levels - step)

    def across_plane(block):
        one, two = swap(block, 1), swap(block, 2)
        half = block.shape[0] // 2
        three = jnp.concatenate([swap(one[:half], 2), swap(two[half:], 1)], 0)
        return [block, one, two, three]

    last_rows = hyena_in[rows - taps :]
    rim = (last_rows[:, 0].astype(jnp.float32) * last_rows[:, 2].astype(jnp.float32)).astype(
        jnp.bfloat16
    )
    rim = lax.ppermute(rim, "ctx", [(i, i + 1) for i in range(n_ctx - 1)])

    def piece(index):
        block = lax.dynamic_slice(attn_in, (0, 0, index * chunk), (rows, 3, chunk))
        return block.transpose(1, 0, 2)

    sent = [piece(me ^ s) for s in range(PLANE)]
    pieces = [sent[0]] + [swap(sent[s], s) for s in range(1, PLANE)]
    attn_rows = attn_weight.reshape(PLANE, chunk, -1)
    attn_weight = jnp.concatenate(
        [lax.dynamic_index_in_dim(attn_rows, me ^ s, 0, False) for s in range(PLANE)], 0
    )
    weights = jnp.stack([out_weight, attn_weight])
    both_up = climb(weights, 1)
    both_down = climb(after(weights, rim), -1)
    product = (hyena_in[:, 0].astype(jnp.float32) * hyena_in[:, 2].astype(jnp.float32)).astype(
        jnp.bfloat16
    )
    product, gate, *pieces = lax.optimization_barrier((product, hyena_in[:, 1], *pieces))

    queries = jnp.stack([p[0] for p in pieces])
    pairs = jnp.stack([p[1:] for p in pieces])
    lower_pairs = move(pairs, 1, 0, levels - 3)
    upper_queries = climb(queries, -1)
    own = attend("causal", True, flags(me, 1), queries, pairs)
    top = levels - 2
    both_up = after(both_up, own[0])
    both_top = move(both_up, 1, top, top)
    hyena_act = fir(after(rim, both_up), product, gate, filters)
    upper_queries = after(upper_queries, hyena_act)
    hyena_one, hyena_two = (swap(after(hyena_act, upper_queries), s) for s in (1, 2))
    carry = attend("full", False, flags(me, 1), upper_queries, pairs)
    both_down = after(both_down, carry[0])
    hyena_down2 = climb(both_down[0], -1, 2)
    lower_pairs = after(lower_pairs, carry[0])
    hyena_rest = move(after(both_up, lower_pairs)[0], 1, 1, top - 1)
    served, served_level = attend(
        "anti", True, flags(me, level > 0), upper_queries, lower_pairs, carry, jnp.bfloat16
    )
    hyena_one, hyena_two, both_top = lax.optimization_barrier(
        (hyena_one, hyena_two, after(both_top, served))
    )
    partial_up = climb(after(served, both_top), 1)
    level_up = climb(after(served_level, both_top), 1)
    half = rows // 2
    hyena_three = swap(hyena_one[:half], 2), swap(after(hyena_two, level_up)[half:], 1)
    hyena_down2 = after(hyena_down2, level_up)
    attn_down2 = climb(after(both_down, hyena_down2)[1], -1, 2)
    hyena_three = jnp.concatenate(lax.optimization_barrier(hyena_three), 0)
    hyena_parts = [hyena_act, hyena_one, hyena_two, hyena_three]
    hyena_up2 = both_top[0] + after(hyena_rest, hyena_three)
    hyena_ups, hyena_downs = [hyena_up2], [hyena_down2]
    attn_ups, attn_downs = [], [attn_down2]
    for step in range(3, levels):
        hyena_ups.append(climb(hyena_ups[-1], 1, step))
    partial_up = after(partial_up, hyena_up2)
    attn_rest = move(after(both_up, partial_up)[1], 1, 1, top - 1)
    attended = across_plane(merge(flags(level > 0), *own, partial_up, level_up))
    for step in range(3, levels):
        hyena_downs.append(climb(after(hyena_downs[-1], attn_downs[0], partial_up), -1, step))
    attn_ups.append(both_top[1] + attn_rest)
    for step in range(3, levels):
        attn_ups.append(climb(attn_ups[-1], 1, step))
        attn_downs.append(climb(after(attn_downs[-1], hyena_downs[-1]), -1, step))
    hyena_weights = hyena_ups[::-1] + [(both_up, 0), (weights, 0), (both_down, 0)] + hyena_downs
    attn_weights = attn_ups[::-1] + [(both_up, 1), (weights, 1), (both_down, 1)] + attn_downs

    def finish(parts, weights):
        mine, others = project(levels, n_tp, flags(level, group), parts, weights)
        total = mine.astype(jnp.float32)
        for shift in range(1, n_tp):
            got = lax.ppermute(
                others[shift - 1], "tp", [(i, (i + shift) % n_tp) for i in range(n_tp)]
            )
            total = total + got.astype(jnp.float32)
        total = total.astype(jnp.bfloat16)
        return assemble(flags(me), [total[0]] + [swap(total[s], s) for s in range(1, PLANE)])

    return (
        finish(hyena_parts, hyena_weights),
        finish(attended, attn_weights),
    )


def solution(mesh):
    in_specs = (
        P("ctx", None, "tp"),
        P(None, "tp"),
        P("ctx", None, "tp"),
        P("tp", "ctx"),
        P("tp", "ctx"),
    )
    out_specs = (P("ctx", "tp"), P("ctx", "tp"))
    return jax.shard_map(
        per_device, mesh=mesh, in_specs=in_specs, out_specs=out_specs, check_vma=False
    )
```

```python
import functools
import math

import jax
import jax.numpy as jnp
import ml_dtypes
import numpy as np
from jax import lax
from jax.experimental import pallas as pl
from jax.experimental.pallas import tpu as pltpu
from jax.sharding import PartitionSpec as P

HEAD_DIM = 128
WINDOW = 2048
PLANE = 4
MASKED = -1e30
LEVEL_ROWS = 16
VMEM = 56 * 1024 * 1024
CHEAP = pl.CostEstimate(flops=1, bytes_accessed=1, transcendentals=0)


def split_bf16(array):
    high = array.astype(jnp.bfloat16)
    return high, (array - high.astype(jnp.float32)).astype(jnp.bfloat16)


def mm(a, b):
    return jnp.dot(a, b, preferred_element_type=jnp.float32)


def dft_matrices(taps):
    size = 2 * taps
    n = np.arange(size)
    k = np.arange(taps)
    angle = 2 * np.pi * ((k[:, None] * n[None, :]) % size) / size
    cosine, sine = np.cos(angle), np.sin(angle)
    forward = np.concatenate([cosine, -sine], 0)
    forward[taps] = (-1.0) ** n
    weight = np.full(taps, 2.0 / size)
    weight[0] = 1.0 / size
    inverse = np.concatenate([cosine * weight[:, None], -sine * weight[:, None]], 0)
    inverse[taps] = (-1.0) ** n / size
    inverse = inverse.T[taps:]

    def halves(array):
        array = array.astype(np.float32)
        high = array.astype(ml_dtypes.bfloat16)
        return high, (array - high.astype(np.float32)).astype(ml_dtypes.bfloat16)

    return [jnp.asarray(m) for m in halves(forward) + halves(inverse)]


def fir_kernel(rim, product, gate, filters, f_hi, f_lo, g_hi, g_lo, out):
    taps = filters.shape[0]
    rows = product.shape[0]
    h_hi, h_lo = split_bf16(filters[...])
    spectrum = (
        mm(f_hi[:, :taps], h_hi) + mm(f_hi[:, :taps], h_lo) + mm(f_lo[:, :taps], h_hi)
    )
    first = lax.broadcasted_iota(jnp.int32, (taps, spectrum.shape[1]), 0) == 0
    h_re, h_im = spectrum[:taps], spectrum[taps:]
    h_re2 = jnp.where(first, h_im, h_re)
    h_im = jnp.where(first, 0.0, h_im)
    for start in range(0, rows, taps):
        before = rim[...] if start == 0 else product[start - taps : start]
        x = jnp.concatenate([before, product[start : start + taps]], 0)
        xs = mm(f_hi[...], x) + mm(f_lo[...], x)
        x_re, x_im = xs[:taps], xs[taps:]
        y = jnp.concatenate([x_re * h_re - x_im * h_im, x_re * h_im + x_im * h_re2], 0)
        y_hi, y_lo = split_bf16(y)
        filtered = mm(g_hi[...], y_hi) + mm(g_hi[...], y_lo) + mm(g_lo[...], y_hi)
        span = slice(start, start + taps)
        out[span] = (gate[span].astype(jnp.float32) * filtered).astype(out.dtype)


def fir(rim, product, gate, filters):
    taps, width = filters.shape
    rows = product.shape[0]
    tile = min(512, width)
    mats = dft_matrices(taps)
    column = lambda n: pl.BlockSpec((n, tile), lambda i: (0, i))
    return pl.pallas_call(
        fir_kernel,
        grid=(width // tile,),
        in_specs=[column(taps), column(rows), column(rows), column(taps)]
        + [pl.BlockSpec(m.shape, lambda i: (0, 0)) for m in mats],
        out_specs=column(rows),
        out_shape=jax.ShapeDtypeStruct((rows, width), jnp.bfloat16),
        compiler_params=pltpu.CompilerParams(vmem_limit_bytes=VMEM),
        cost_estimate=CHEAP,
    )(rim, product, gate, filters, *mats)


def pack_level(level):
    pieces, rest = [], level
    for _ in range(3):
        term = rest.astype(jnp.bfloat16).astype(jnp.float32)
        pieces += [term[:, c : c + HEAD_DIM] for c in range(0, level.shape[1], HEAD_DIM)]
        rest = rest - term
    pieces += [jnp.zeros((LEVEL_ROWS - len(pieces), HEAD_DIM), jnp.float32)]
    return jnp.concatenate(pieces, 0).astype(jnp.bfloat16)


def unpack_level(block, rows):
    block = block.astype(jnp.float32)
    count = rows // HEAD_DIM
    total = block[0:count] + block[count : 2 * count] + block[2 * count : 3 * count]
    return jnp.concatenate([total[c : c + 1] for c in range(count)], 1)


def attend_kernel(kind, first, last, info, q_ref, k_ref, v_ref, *refs):
    refs = list(refs)
    if not first:
        acc_in, stat_in = refs.pop(0), refs.pop(0)
    packed = len(refs) == 1
    out, stat_out = refs[0], refs[-1]
    plane, rows = k_ref.shape[0], k_ref.shape[2]
    me = info[0]
    factor = math.log2(math.e) / math.sqrt(HEAD_DIM)
    half = HEAD_DIM // 2

    def write(i, top, total, acc):
        if last:
            out[me ^ i, :rows] = (acc * (1.0 / total)).astype(out.dtype)
            level = jnp.broadcast_to(top + jnp.log2(total), (rows, HEAD_DIM)).T[0:1]
            if packed:
                out[me ^ i, rows:] = pack_level(level)
            else:
                stat_out[0, me ^ i] = jnp.broadcast_to(level, (8, rows))
        else:
            out[me ^ i] = acc
            lane = lax.broadcasted_iota(jnp.int32, (rows, HEAD_DIM), 1)
            stat_out[me ^ i] = jnp.where(lane < half, top, total)

    def previous(i):
        stat = stat_in[me ^ i]
        return stat[:, 0:1], stat[:, half : half + 1], acc_in[me ^ i]

    def attend(i):
        blocks = range(plane)
        if kind != "full":
            blocks = range(i + 1) if kind == "causal" else range(i, plane)
        q = q_ref[me ^ i]
        scores = []
        for j in blocks:
            s = lax.dot_general(
                q, k_ref[me ^ j, 0], (((1,), (1,)), ((), ())), preferred_element_type=jnp.float32
            ) * factor
            if j == i and kind != "full":
                row = lax.broadcasted_iota(jnp.int32, s.shape, 0)
                col = lax.broadcasted_iota(jnp.int32, s.shape, 1)
                s = jnp.where(col <= row if kind == "causal" else col > row, s, MASKED)
            scores.append(s)
        top = functools.reduce(jnp.maximum, scores).max(axis=1, keepdims=True)
        if not first:
            old_top, old_total, old_acc = previous(i)
            top = jnp.maximum(top, old_top)
        acc, sums = None, None
        for j, s in zip(blocks, scores):
            w = jnp.exp2(s - top)
            sums = w if sums is None else sums + w
            term = mm(w.astype(jnp.bfloat16), v_ref[me ^ j, 0])
            acc = term if acc is None else acc + term
        total = sums.sum(axis=1, keepdims=True)
        if not first:
            shrink = jnp.exp2(old_top - top)
            total = total + shrink * old_total
            acc = acc + shrink * old_acc
        write(i, top, total, acc)

    def run():
        for i in range(plane):
            attend(i)

    if first:
        run()
    else:

        @pl.when(info[1] > 0)
        def _():
            run()

        @pl.when(info[1] == 0)
        def _():
            for i in range(plane):
                write(i, *previous(i))


def attend(kind, last, info, queries, pairs, carry=(), dtype=jnp.float32):
    plane, rows, width = queries.shape
    heads = width // HEAD_DIM
    mine = pl.BlockSpec((plane, rows, HEAD_DIM), lambda h, info: (0, 0, h))
    keys = pl.BlockSpec((plane, 1, rows, HEAD_DIM), lambda h, info: (0, 0, 0, h))
    values = pl.BlockSpec((plane, 1, rows, HEAD_DIM), lambda h, info: (0, 1, 0, h))
    state = jax.ShapeDtypeStruct(queries.shape, jnp.float32)
    if last and dtype == jnp.bfloat16:
        tall = (plane, rows + LEVEL_ROWS)
        out_specs = pl.BlockSpec(tall + (HEAD_DIM,), lambda h, info: (0, 0, h))
        out_shape = jax.ShapeDtypeStruct(tall + (width,), dtype)
    elif last:
        out_specs = (mine, pl.BlockSpec((1, plane, 8, rows), lambda h, info: (h, 0, 0, 0)))
        out_shape = (
            jax.ShapeDtypeStruct(queries.shape, dtype),
            jax.ShapeDtypeStruct((heads, plane, 8, rows), jnp.float32),
        )
    else:
        out_specs, out_shape = (mine, mine), (state, state)
    return pl.pallas_call(
        functools.partial(attend_kernel, kind, not carry, last),
        grid_spec=pltpu.PrefetchScalarGridSpec(
            num_scalar_prefetch=1,
            grid=(heads,),
            in_specs=[mine, keys, values] + [mine] * len(carry),
            out_specs=out_specs,
        ),
        out_shape=out_shape,
        compiler_params=pltpu.CompilerParams(vmem_limit_bytes=VMEM),
        cost_estimate=CHEAP,
    )(info, queries, pairs, pairs, *carry)


def merge_kernel(info, one_ref, level_one, two_ref, out):
    rows = one_ref.shape[1]
    for h in range(one_ref.shape[2] // HEAD_DIM):
        span = slice(h * HEAD_DIM, (h + 1) * HEAD_DIM)
        one, two = level_one[h, 0, 0:1], unpack_level(two_ref[0, rows:, span], rows)
        two = jnp.where(info[0] > 0, two, MASKED)
        top = jnp.maximum(one, two)
        one, two = jnp.exp2(one - top), jnp.exp2(two - top)
        share = jnp.broadcast_to(two * (1.0 / (one + two)), (HEAD_DIM, rows)).T
        first, second = one_ref[0, :, span], two_ref[0, :rows, span].astype(jnp.float32)
        out[0, :, span] = (first + share * (second - first)).astype(out.dtype)


def merge(info, one, level_one, two):
    plane, rows, width = one.shape
    block = pl.BlockSpec((1, rows, width), lambda i, info: (i, 0, 0))
    level = pl.BlockSpec((level_one.shape[0], 1, 8, rows), lambda i, info: (0, i, 0, 0))
    return pl.pallas_call(
        merge_kernel,
        grid_spec=pltpu.PrefetchScalarGridSpec(
            num_scalar_prefetch=1,
            grid=(plane,),
            in_specs=[
                block,
                level,
                pl.BlockSpec((1,) + two.shape[1:], lambda i, info: (i, 0, 0)),
            ],
            out_specs=block,
        ),
        out_shape=jax.ShapeDtypeStruct(one.shape, jnp.bfloat16),
        compiler_params=pltpu.CompilerParams(vmem_limit_bytes=VMEM),
        cost_estimate=CHEAP,
    )(info, one, level_one, two)


def project_kernel(levels, n_tp, part_index, weight_index, info, *refs):
    splits = len(part_index)
    parts, weights = refs[:splits], refs[splits:-8]
    mine, others, a, w, y, sem_a, sem_w, sem_y = refs[-8:]
    level, group = info[0], info[1]
    plane, rows, columns = y.shape[1:]
    depth = a.shape[1] // plane
    share = levels // n_tp

    loads = []
    for s, (part, index) in enumerate(zip(parts, part_index)):
        if index is not None:
            copy = pltpu.make_async_copy(part.at[index], a.at[pl.ds(s * rows, rows)], sem_a.at[s])
            loads.append(copy)
            continue
        for r in range(plane):
            loads.append(
                pltpu.make_async_copy(
                    part.at[r ^ s],
                    a.at[pl.ds(r * rows, rows), pl.ds(s * depth, depth)],
                    sem_a.at[s * plane + r],
                )
            )
    for copy in loads:
        copy.start()
    for position, (weight, index) in enumerate(zip(weights, weight_index)):
        target = level + (position - (levels - 1))

        @pl.when((target >= 0) & (target < levels))
        def _(weight=weight, index=index, target=target):
            pltpu.make_async_copy(weight.at[index], w.at[target], sem_w.at[target]).start()

    def store(t, act):
        ahead = (t // share + n_tp - group) % n_tp

        @pl.when(ahead == 0)
        def _():
            act(pltpu.make_async_copy(y.at[t], mine.at[:, t % share], sem_y.at[t]))

        @pl.when(ahead > 0)
        def _():
            act(pltpu.make_async_copy(y.at[t], others.at[ahead - 1, :, t % share], sem_y.at[t]))

    for copy in loads:
        copy.wait()
    for t in range(levels):
        pltpu.make_async_copy(weights[0].at[0], w.at[t], sem_w.at[t]).wait()
        for r in range(plane):
            y[t, r] = mm(a[r * rows : (r + 1) * rows], w[t]).astype(y.dtype)
        store(t, lambda copy: copy.start())
    for t in range(levels):
        store(t, lambda copy: copy.wait())


def project(levels, n_tp, info, parts, weights):
    parts = [p if isinstance(p, tuple) else (p, None) for p in parts]
    weights = [w if isinstance(w, tuple) else (w[None], 0) for w in weights]
    width, columns = weights[0][0].shape[1:]
    rows = parts[0][0].shape[1]
    block = (PLANE, levels // n_tp, rows, columns)
    anywhere = pl.BlockSpec(memory_space=pl.ANY)
    return pl.pallas_call(
        functools.partial(
            project_kernel, levels, n_tp, [i for _, i in parts], [i for _, i in weights]
        ),
        grid_spec=pltpu.PrefetchScalarGridSpec(
            num_scalar_prefetch=1,
            grid=(1,),
            in_specs=[anywhere] * (len(parts) + len(weights)),
            out_specs=(anywhere, anywhere),
            scratch_shapes=[
                pltpu.VMEM((PLANE * rows, width), jnp.bfloat16),
                pltpu.VMEM((levels, width, columns), jnp.bfloat16),
                pltpu.VMEM((levels, PLANE, rows, columns), jnp.bfloat16),
                pltpu.SemaphoreType.DMA((PLANE * PLANE,)),
                pltpu.SemaphoreType.DMA((levels,)),
                pltpu.SemaphoreType.DMA((levels,)),
            ],
        ),
        out_shape=(
            jax.ShapeDtypeStruct(block, jnp.bfloat16),
            jax.ShapeDtypeStruct((n_tp - 1,) + block, jnp.bfloat16),
        ),
        compiler_params=pltpu.CompilerParams(vmem_limit_bytes=VMEM),
        cost_estimate=CHEAP,
    )(info, *[p for p, _ in parts], *[w for w, _ in weights])


def assemble_kernel(info, *refs):
    pieces, out = refs[:-1], refs[-1]
    share, rows, columns = pieces[0].shape
    for s, piece in enumerate(pieces):
        for t in range(share):
            start = pl.multiple_of((t * PLANE + (info[0] ^ s)) * columns, columns)
            out[:, pl.ds(start, columns)] = piece[t]


def assemble(info, pieces):
    share, rows, columns = pieces[0].shape
    if columns % 128:
        natural = [
            lax.select_n(info[0], *[pieces[t ^ j] for t in range(PLANE)]) for j in range(PLANE)
        ]
        return jnp.stack(natural, 1).transpose(2, 0, 1, 3).reshape(rows, -1)
    return pl.pallas_call(
        assemble_kernel,
        grid_spec=pltpu.PrefetchScalarGridSpec(
            num_scalar_prefetch=1,
            grid=(1,),
            in_specs=[pl.BlockSpec(p.shape, lambda i, info: (0, 0, 0)) for p in pieces],
            out_specs=pl.BlockSpec((rows, share * PLANE * columns), lambda i, info: (0, 0)),
        ),
        out_shape=jax.ShapeDtypeStruct((rows, share * PLANE * columns), jnp.bfloat16),
        compiler_params=pltpu.CompilerParams(vmem_limit_bytes=VMEM),
        cost_estimate=CHEAP,
    )(info, *pieces)


def per_device(hyena_in, filters, attn_in, out_weight, attn_weight):
    rows, _, width = hyena_in.shape
    taps = filters.shape[0]
    n_ctx, n_tp = lax.axis_size("ctx"), lax.axis_size("tp")
    levels = n_ctx // PLANE
    device_index = lax.axis_index("ctx")
    group = lax.axis_index("tp")
    me, level = device_index % PLANE, device_index // PLANE
    chunk = width // PLANE
    assert WINDOW == 2 * PLANE * rows and levels > 2 and levels % n_tp == 0

    def flags(*values):
        return jnp.stack([jnp.asarray(v).astype(jnp.int32) for v in values])

    def after(value, *others):
        return lax.optimization_barrier((value, *others))[0]

    def swap(block, relative):
        return lax.ppermute(block, "ctx", [(i, i ^ relative) for i in range(n_ctx)])

    def move(block, direction, first, last):
        sources = range(first * PLANE, (last + 1) * PLANE)
        return lax.ppermute(block, "ctx", [(i, i + direction * PLANE) for i in sources])

    def climb(block, direction, step=1):
        if direction > 0:
            return move(block, 1, step - 1, levels - 2)
        return move(block, -1, 1, levels - step)

    def across_plane(block):
        one, two = swap(block, 1), swap(block, 2)
        half = block.shape[0] // 2
        three = jnp.concatenate([swap(one[:half], 2), swap(two[half:], 1)], 0)
        return [block, one, two, three]

    last_rows = hyena_in[rows - taps :]
    rim = (last_rows[:, 0].astype(jnp.float32) * last_rows[:, 2].astype(jnp.float32)).astype(
        jnp.bfloat16
    )
    attn_rows = attn_weight.reshape(PLANE, chunk, -1)
    attn_weight = jnp.concatenate(
        [lax.dynamic_index_in_dim(attn_rows, me ^ s, 0, False) for s in range(PLANE)], 0
    )
    weights = after(jnp.stack([out_weight, attn_weight]), rim)
    attn_in = after(attn_in, weights)
    rim = lax.ppermute(rim, "ctx", [(i, i + 1) for i in range(n_ctx - 1)])

    def piece(index):
        block = lax.dynamic_slice(attn_in, (0, 0, index * chunk), (rows, 3, chunk))
        return block.transpose(1, 0, 2)

    sent = list(lax.optimization_barrier([piece(me ^ s) for s in range(PLANE)]))
    pieces = [sent[0]] + [swap(sent[s], s) for s in range(1, PLANE)]
    both_up = climb(weights, 1)
    both_down = climb(after(weights, rim), -1)
    product = (hyena_in[:, 0].astype(jnp.float32) * hyena_in[:, 2].astype(jnp.float32)).astype(
        jnp.bfloat16
    )
    hyena_act = fir(rim, product, hyena_in[:, 1], filters)
    hyena_act, *pieces = lax.optimization_barrier((hyena_act, *pieces))

    pairs = jnp.stack([p[1:] for p in pieces])
    queries = jnp.stack([p[0] for p in lax.optimization_barrier([pairs] + pieces)[1:]])
    lower_pairs = move(pairs, 1, 0, levels - 3)
    upper_queries = climb(queries, -1)
    hyena_one = swap(after(hyena_act, queries), 1)
    own = attend("causal", True, flags(me, 1), queries, pairs)
    top = levels - 2
    both_up = after(both_up, own[0])
    both_top = move(both_up, 1, top, top)
    hyena_rest, attn_rest = lax.optimization_barrier((both_up[0], both_up[1]))
    upper_queries, both_down, hyena_one = lax.optimization_barrier(
        (after(upper_queries, hyena_rest), both_down, hyena_one)
    )
    hyena_rest = move(after(hyena_rest, upper_queries), 1, 1, top - 1)
    hyena_down2 = climb(both_down[0], -1, 2)
    hyena_pair = jnp.stack([hyena_act, hyena_one])
    hyena_other = swap(hyena_pair, 2)
    carry = attend("full", False, flags(me, 1), upper_queries, pairs)
    lower_pairs, attn_down2 = lax.optimization_barrier((after(lower_pairs, carry[0]), both_down[1]))
    attn_down2 = climb(attn_down2, -1, 2)
    served = attend(
        "anti", True, flags(me, level > 0), upper_queries, lower_pairs, carry, jnp.bfloat16
    )
    served, both_top, hyena_down2 = lax.optimization_barrier((served, both_top, hyena_down2))
    partial_up = climb(served, 1)
    attn_rest = move(after(attn_rest, served), 1, 1, top - 1)
    hyena_up2 = both_top[0] + after(hyena_rest, served)
    hyena_ups, hyena_downs = [hyena_up2], [hyena_down2]
    attn_ups, attn_downs = [], [attn_down2]
    for step in range(3, levels):
        hyena_ups.append(climb(hyena_ups[-1], 1, step))
        hyena_downs.append(climb(after(hyena_downs[-1], attn_down2), -1, step))
    attended = merge(flags(level > 0), *own, after(partial_up, hyena_up2, hyena_other))
    attn_ups.append(both_top[1] + after(attn_rest, attended, hyena_ups[-1], hyena_downs[-1]))
    for step in range(3, levels):
        attn_ups.append(climb(attn_ups[-1], 1, step))
        attn_downs.append(climb(after(attn_downs[-1], hyena_downs[-1]), -1, step))
    hyena_parts = [(hyena_pair, 0), (hyena_pair, 1), (hyena_other, 0), (hyena_other, 1)]
    hyena_weights = hyena_ups[::-1] + [(both_up, 0), (weights, 0), (both_down, 0)] + hyena_downs

    def add_up(mine, others):
        gots = [
            lax.ppermute(others[shift - 1], "tp", [(i, (i + shift) % n_tp) for i in range(n_tp)])
            for shift in range(1, n_tp)
        ]
        pieces = []
        for s in range(PLANE):
            total = mine[s].astype(jnp.float32)
            for got in gots:
                total = total + got[s].astype(jnp.float32)
            pieces.append(total.astype(jnp.bfloat16))
        return pieces

    def exchange(pieces):
        return [pieces[0]] + [swap(pieces[s], s) for s in range(1, PLANE)]

    where = flags(level, group)
    attn_one, attn_two = swap(attended, 1), swap(attended, 2)
    hyena_terms = project(levels, n_tp, where, hyena_parts, hyena_weights)
    attn_one, attn_two, *hyena_terms = lax.optimization_barrier(
        (after(attn_one, attn_ups[0]), attn_two, *hyena_terms)
    )
    half = PLANE // 2
    attn_three = [swap(attn_one[:half], 2), swap(attn_two[half:], 1)]
    hyena_pieces = add_up(*hyena_terms)
    attn_three, attn_ups[-1], attn_downs[-1], *hyena_pieces = lax.optimization_barrier(
        (jnp.concatenate(attn_three, 0), attn_ups[-1], attn_downs[-1], *hyena_pieces)
    )
    hyena_pieces = exchange(hyena_pieces)
    attn_weights = attn_ups[::-1] + [(both_up, 1), (weights, 1), (both_down, 1)] + attn_downs
    attn_parts = [attended, attn_one, attn_two, attn_three]
    attn_terms = project(levels, n_tp, where, attn_parts, attn_weights)
    hyena_pieces = [after(p, *attn_terms) for p in hyena_pieces]
    attn_pieces = exchange(add_up(*attn_terms))
    return assemble(flags(me), hyena_pieces), assemble(flags(me), attn_pieces)


def solution(mesh):
    in_specs = (
        P("ctx", None, "tp"),
        P(None, "tp"),
        P("ctx", None, "tp"),
        P("tp", "ctx"),
        P("tp", "ctx"),
    )
    out_specs = (P("ctx", "tp"), P("ctx", "tp"))
    return jax.shard_map(
        per_device, mesh=mesh, in_specs=in_specs, out_specs=out_specs, check_vma=False
    )
```

```python
import functools
import math

import jax
import jax.numpy as jnp
import ml_dtypes
import numpy as np
from jax import lax
from jax.experimental import pallas as pl
from jax.experimental.pallas import tpu as pltpu
from jax.sharding import PartitionSpec as P

HEAD_DIM = 128
WINDOW = 2048
PLANE = 4
MASKED = -1e30
LEVEL_ROWS = 16
VMEM = 56 * 1024 * 1024
CHEAP = pl.CostEstimate(flops=1, bytes_accessed=1, transcendentals=0)
MODEST = pl.CostEstimate(flops=2 * 10**9, bytes_accessed=1, transcendentals=0)
LARGE = pl.CostEstimate(flops=10**10, bytes_accessed=1, transcendentals=0)
ATTEND_COST = {"causal": LARGE, "full": CHEAP, "anti": LARGE}


def split_bf16(array):
    high = array.astype(jnp.bfloat16)
    return high, (array - high.astype(jnp.float32)).astype(jnp.bfloat16)


def mm(a, b):
    return jnp.dot(a, b, preferred_element_type=jnp.float32)


def dft_matrices(taps):
    size = 2 * taps
    n = np.arange(size)
    k = np.arange(taps)
    angle = 2 * np.pi * ((k[:, None] * n[None, :]) % size) / size
    cosine, sine = np.cos(angle), np.sin(angle)
    forward = np.concatenate([cosine, -sine], 0)
    forward[taps] = (-1.0) ** n
    weight = np.full(taps, 2.0 / size)
    weight[0] = 1.0 / size
    inverse = np.concatenate([cosine * weight[:, None], -sine * weight[:, None]], 0)
    inverse[taps] = (-1.0) ** n / size
    inverse = inverse.T[taps:]

    def halves(array):
        array = array.astype(np.float32)
        high = array.astype(ml_dtypes.bfloat16)
        return high, (array - high.astype(np.float32)).astype(ml_dtypes.bfloat16)

    return [jnp.asarray(m) for m in halves(forward) + halves(inverse)]


def fir_kernel(rim, product, gate, filters, f_hi, f_lo, g_hi, g_lo, out):
    taps = filters.shape[0]
    rows = product.shape[0]
    h_hi, h_lo = split_bf16(filters[...])
    spectrum = (
        mm(f_hi[:, :taps], h_hi) + mm(f_hi[:, :taps], h_lo) + mm(f_lo[:, :taps], h_hi)
    )
    first = lax.broadcasted_iota(jnp.int32, (taps, spectrum.shape[1]), 0) == 0
    h_re, h_im = spectrum[:taps], spectrum[taps:]
    h_re2 = jnp.where(first, h_im, h_re)
    h_im = jnp.where(first, 0.0, h_im)
    for start in range(0, rows, taps):
        before = rim[...] if start == 0 else product[start - taps : start]
        x = jnp.concatenate([before, product[start : start + taps]], 0)
        xs = mm(f_hi[...], x) + mm(f_lo[...], x)
        x_re, x_im = xs[:taps], xs[taps:]
        y = jnp.concatenate([x_re * h_re - x_im * h_im, x_re * h_im + x_im * h_re2], 0)
        y_hi, y_lo = split_bf16(y)
        filtered = mm(g_hi[...], y_hi) + mm(g_hi[...], y_lo) + mm(g_lo[...], y_hi)
        span = slice(start, start + taps)
        out[span] = (gate[span].astype(jnp.float32) * filtered).astype(out.dtype)


@jax.named_scope('fir')
def fir(rim, product, gate, filters):
    taps, width = filters.shape
    rows = product.shape[0]
    tile = min(512, width)
    mats = dft_matrices(taps)
    column = lambda n: pl.BlockSpec((n, tile), lambda i: (0, i))
    return pl.pallas_call(
        fir_kernel,
        grid=(width // tile,),
        in_specs=[column(taps), column(rows), column(rows), column(taps)]
        + [pl.BlockSpec(m.shape, lambda i: (0, 0)) for m in mats],
        out_specs=column(rows),
        out_shape=jax.ShapeDtypeStruct((rows, width), jnp.bfloat16),
        compiler_params=pltpu.CompilerParams(vmem_limit_bytes=VMEM),
        cost_estimate=CHEAP,
    )(rim, product, gate, filters, *mats)


def pack_level(level):
    pieces, rest = [], level
    for _ in range(3):
        term = rest.astype(jnp.bfloat16).astype(jnp.float32)
        pieces += [term[:, c : c + HEAD_DIM] for c in range(0, level.shape[1], HEAD_DIM)]
        rest = rest - term
    pieces += [jnp.zeros((LEVEL_ROWS - len(pieces), HEAD_DIM), jnp.float32)]
    return jnp.concatenate(pieces, 0).astype(jnp.bfloat16)


def unpack_level(block, rows):
    block = block.astype(jnp.float32)
    count = rows // HEAD_DIM
    total = block[0:count] + block[count : 2 * count] + block[2 * count : 3 * count]
    return jnp.concatenate([total[c : c + 1] for c in range(count)], 1)


def attend_kernel(kind, first, last, info, q_ref, k_ref, v_ref, *refs):
    refs = list(refs)
    if not first:
        acc_in, stat_in = refs.pop(0), refs.pop(0)
    packed = len(refs) == 1
    out, stat_out = refs[0], refs[-1]
    plane, rows = k_ref.shape[0], k_ref.shape[2]
    me = info[0]
    factor = math.log2(math.e) / math.sqrt(HEAD_DIM)
    half = HEAD_DIM // 2

    def write(i, top, total, acc):
        if last:
            out[me ^ i, :rows] = (acc * (1.0 / total)).astype(out.dtype)
            level = jnp.broadcast_to(top + jnp.log2(total), (rows, HEAD_DIM)).T[0:1]
            if packed:
                out[me ^ i, rows:] = pack_level(level)
            else:
                stat_out[0, me ^ i] = jnp.broadcast_to(level, (8, rows))
        else:
            out[me ^ i] = acc
            lane = lax.broadcasted_iota(jnp.int32, (rows, HEAD_DIM), 1)
            stat_out[me ^ i] = jnp.where(lane < half, top, total)

    def previous(i):
        stat = stat_in[me ^ i]
        return stat[:, 0:1], stat[:, half : half + 1], acc_in[me ^ i]

    def attend(i):
        blocks = range(plane)
        if kind != "full":
            blocks = range(i + 1) if kind == "causal" else range(i, plane)
        q = q_ref[me ^ i]
        scores = []
        for j in blocks:
            s = lax.dot_general(
                q, k_ref[me ^ j, 0], (((1,), (1,)), ((), ())), preferred_element_type=jnp.float32
            ) * factor
            if j == i and kind != "full":
                row = lax.broadcasted_iota(jnp.int32, s.shape, 0)
                col = lax.broadcasted_iota(jnp.int32, s.shape, 1)
                s = jnp.where(col <= row if kind == "causal" else col > row, s, MASKED)
            scores.append(s)
        top = functools.reduce(jnp.maximum, scores).max(axis=1, keepdims=True)
        if not first:
            old_top, old_total, old_acc = previous(i)
            top = jnp.maximum(top, old_top)
        acc, sums = None, None
        for j, s in zip(blocks, scores):
            w = jnp.exp2(s - top)
            sums = w if sums is None else sums + w
            term = mm(w.astype(jnp.bfloat16), v_ref[me ^ j, 0])
            acc = term if acc is None else acc + term
        total = sums.sum(axis=1, keepdims=True)
        if not first:
            shrink = jnp.exp2(old_top - top)
            total = total + shrink * old_total
            acc = acc + shrink * old_acc
        write(i, top, total, acc)

    def run():
        for i in range(plane):
            attend(i)

    if first:
        run()
    else:

        @pl.when(info[1] > 0)
        def _():
            run()

        @pl.when(info[1] == 0)
        def _():
            for i in range(plane):
                write(i, *previous(i))


def attend(kind, last, info, queries, pairs, carry=(), dtype=jnp.float32):
    plane, rows, width = queries.shape
    heads = width // HEAD_DIM
    mine = pl.BlockSpec((plane, rows, HEAD_DIM), lambda h, info: (0, 0, h))
    keys = pl.BlockSpec((plane, 1, rows, HEAD_DIM), lambda h, info: (0, 0, 0, h))
    values = pl.BlockSpec((plane, 1, rows, HEAD_DIM), lambda h, info: (0, 1, 0, h))
    state = jax.ShapeDtypeStruct(queries.shape, jnp.float32)
    if last and dtype == jnp.bfloat16:
        tall = (plane, rows + LEVEL_ROWS)
        out_specs = pl.BlockSpec(tall + (HEAD_DIM,), lambda h, info: (0, 0, h))
        out_shape = jax.ShapeDtypeStruct(tall + (width,), dtype)
    elif last:
        out_specs = (mine, pl.BlockSpec((1, plane, 8, rows), lambda h, info: (h, 0, 0, 0)))
        out_shape = (
            jax.ShapeDtypeStruct(queries.shape, dtype),
            jax.ShapeDtypeStruct((heads, plane, 8, rows), jnp.float32),
        )
    else:
        out_specs, out_shape = (mine, mine), (state, state)
    return pl.pallas_call(
        functools.partial(attend_kernel, kind, not carry, last),
        grid_spec=pltpu.PrefetchScalarGridSpec(
            num_scalar_prefetch=1,
            grid=(heads,),
            in_specs=[mine, keys, values] + [mine] * len(carry),
            out_specs=out_specs,
        ),
        out_shape=out_shape,
        compiler_params=pltpu.CompilerParams(vmem_limit_bytes=VMEM),
        cost_estimate=ATTEND_COST[kind],
    )(info, queries, pairs, pairs, *carry)


def merge_kernel(info, one_ref, level_one, two_ref, out):
    rows = one_ref.shape[1]
    for h in range(one_ref.shape[2] // HEAD_DIM):
        span = slice(h * HEAD_DIM, (h + 1) * HEAD_DIM)
        one, two = level_one[h, 0, 0:1], unpack_level(two_ref[0, rows:, span], rows)
        two = jnp.where(info[0] > 0, two, MASKED)
        top = jnp.maximum(one, two)
        one, two = jnp.exp2(one - top), jnp.exp2(two - top)
        share = jnp.broadcast_to(two * (1.0 / (one + two)), (HEAD_DIM, rows)).T
        first, second = one_ref[0, :, span], two_ref[0, :rows, span].astype(jnp.float32)
        out[0, :, span] = (first + share * (second - first)).astype(out.dtype)


@jax.named_scope('merge')
def merge(info, one, level_one, two):
    plane, rows, width = one.shape
    block = pl.BlockSpec((1, rows, width), lambda i, info: (i, 0, 0))
    level = pl.BlockSpec((level_one.shape[0], 1, 8, rows), lambda i, info: (0, i, 0, 0))
    return pl.pallas_call(
        merge_kernel,
        grid_spec=pltpu.PrefetchScalarGridSpec(
            num_scalar_prefetch=1,
            grid=(plane,),
            in_specs=[
                block,
                level,
                pl.BlockSpec((1,) + two.shape[1:], lambda i, info: (i, 0, 0)),
            ],
            out_specs=block,
        ),
        out_shape=jax.ShapeDtypeStruct(one.shape, jnp.bfloat16),
        compiler_params=pltpu.CompilerParams(vmem_limit_bytes=VMEM),
        cost_estimate=MODEST,
    )(info, one, level_one, two)


def project_kernel(levels, n_tp, part_index, weight_index, info, *refs):
    splits = len(part_index)
    parts, weights = refs[:splits], refs[splits:-8]
    mine, others, a, w, y, sem_a, sem_w, sem_y = refs[-8:]
    level, group = info[0], info[1]
    plane, rows, columns = y.shape[1:]
    depth = a.shape[1] // plane
    share = levels // n_tp

    loads = []
    for s, (part, index) in enumerate(zip(parts, part_index)):
        if index is not None:
            copy = pltpu.make_async_copy(part.at[index], a.at[pl.ds(s * rows, rows)], sem_a.at[s])
            loads.append(copy)
            continue
        for r in range(plane):
            loads.append(
                pltpu.make_async_copy(
                    part.at[r ^ s],
                    a.at[pl.ds(r * rows, rows), pl.ds(s * depth, depth)],
                    sem_a.at[s * plane + r],
                )
            )
    for copy in loads:
        copy.start()
    for weight, (index, offset, first, last) in zip(weights, weight_index):
        target = level + offset

        @pl.when((level >= first) & (level <= last))
        def _(weight=weight, index=index, target=target):
            pltpu.make_async_copy(weight.at[index], w.at[target], sem_w.at[target]).start()

    def store(t, act):
        ahead = (t // share + n_tp - group) % n_tp

        @pl.when(ahead == 0)
        def _():
            act(pltpu.make_async_copy(y.at[t], mine.at[:, t % share], sem_y.at[t]))

        @pl.when(ahead > 0)
        def _():
            act(pltpu.make_async_copy(y.at[t], others.at[ahead - 1, :, t % share], sem_y.at[t]))

    for copy in loads:
        copy.wait()
    for t in range(levels):
        pltpu.make_async_copy(weights[0].at[0], w.at[t], sem_w.at[t]).wait()
        for r in range(plane):
            y[t, r] = mm(a[r * rows : (r + 1) * rows], w[t]).astype(y.dtype)
        store(t, lambda copy: copy.start())
    for t in range(levels):
        store(t, lambda copy: copy.wait())


@jax.named_scope('project')
def project(levels, n_tp, info, parts, weights, cost=CHEAP):
    parts = [p if isinstance(p, tuple) else (p, None) for p in parts]
    weights = [(w[0][None], 0, *w[2:]) if w[0].ndim == 2 else w for w in weights]
    width, columns = weights[0][0].shape[1:]
    rows = parts[0][0].shape[1]
    block = (PLANE, levels // n_tp, rows, columns)
    anywhere = pl.BlockSpec(memory_space=pl.ANY)
    return pl.pallas_call(
        functools.partial(
            project_kernel, levels, n_tp, [i for _, i in parts], [w[1:] for w in weights]
        ),
        grid_spec=pltpu.PrefetchScalarGridSpec(
            num_scalar_prefetch=1,
            grid=(1,),
            in_specs=[anywhere] * (len(parts) + len(weights)),
            out_specs=(anywhere, anywhere),
            scratch_shapes=[
                pltpu.VMEM((PLANE * rows, width), jnp.bfloat16),
                pltpu.VMEM((levels, width, columns), jnp.bfloat16),
                pltpu.VMEM((levels, PLANE, rows, columns), jnp.bfloat16),
                pltpu.SemaphoreType.DMA((PLANE * PLANE,)),
                pltpu.SemaphoreType.DMA((levels,)),
                pltpu.SemaphoreType.DMA((levels,)),
            ],
        ),
        out_shape=(
            jax.ShapeDtypeStruct(block, jnp.bfloat16),
            jax.ShapeDtypeStruct((n_tp - 1,) + block, jnp.bfloat16),
        ),
        compiler_params=pltpu.CompilerParams(vmem_limit_bytes=VMEM),
        cost_estimate=cost,
    )(info, *[p for p, _ in parts], *[w[0] for w in weights])


def assemble_kernel(info, *refs):
    pieces, out = refs[:-1], refs[-1]
    share, rows, columns = pieces[0].shape
    for s, piece in enumerate(pieces):
        for t in range(share):
            start = pl.multiple_of((t * PLANE + (info[0] ^ s)) * columns, columns)
            out[:, pl.ds(start, columns)] = piece[t]


@jax.named_scope('assemble')
def assemble(info, pieces):
    share, rows, columns = pieces[0].shape
    if columns % 128:
        natural = [
            lax.select_n(info[0], *[pieces[t ^ j] for t in range(PLANE)]) for j in range(PLANE)
        ]
        return jnp.stack(natural, 1).transpose(2, 0, 1, 3).reshape(rows, -1)
    return pl.pallas_call(
        assemble_kernel,
        grid_spec=pltpu.PrefetchScalarGridSpec(
            num_scalar_prefetch=1,
            grid=(1,),
            in_specs=[pl.BlockSpec(p.shape, lambda i, info: (0, 0, 0)) for p in pieces],
            out_specs=pl.BlockSpec((rows, share * PLANE * columns), lambda i, info: (0, 0)),
        ),
        out_shape=jax.ShapeDtypeStruct((rows, share * PLANE * columns), jnp.bfloat16),
        compiler_params=pltpu.CompilerParams(vmem_limit_bytes=VMEM),
        cost_estimate=CHEAP,
    )(info, *pieces)


def per_device(hyena_in, filters, attn_in, out_weight, attn_weight):
    rows, _, width = hyena_in.shape
    taps = filters.shape[0]
    n_ctx, n_tp = lax.axis_size("ctx"), lax.axis_size("tp")
    levels = n_ctx // PLANE
    device_index = lax.axis_index("ctx")
    group = lax.axis_index("tp")
    me, level = device_index % PLANE, device_index // PLANE
    chunk = width // PLANE
    assert WINDOW == 2 * PLANE * rows and levels > 2 and levels % n_tp == 0

    def flags(*values):
        return jnp.stack([jnp.asarray(v).astype(jnp.int32) for v in values])

    def after(value, *others):
        return lax.optimization_barrier((value, *others))[0]

    def swap(block, relative):
        return lax.ppermute(block, "ctx", [(i, i ^ relative) for i in range(n_ctx)])

    def move(block, direction, first, last):
        sources = range(first * PLANE, (last + 1) * PLANE)
        return lax.ppermute(block, "ctx", [(i, i + direction * PLANE) for i in sources])

    def climb(block, direction, step=1):
        if direction > 0:
            return move(block, 1, step - 1, levels - 2)
        return move(block, -1, 1, levels - step)

    last_rows = hyena_in[rows - taps :]
    rim = (last_rows[:, 0].astype(jnp.float32) * last_rows[:, 2].astype(jnp.float32)).astype(
        jnp.bfloat16
    )
    attn_rows = attn_weight.reshape(PLANE, chunk, -1)
    attn_weight = jnp.concatenate(
        [lax.dynamic_index_in_dim(attn_rows, me ^ s, 0, False) for s in range(PLANE)], 0
    )
    weights = after(jnp.stack([out_weight, attn_weight]), rim)
    attn_in = after(attn_in, weights)
    rim = lax.ppermute(rim, "ctx", [(i, i + 1) for i in range(n_ctx - 1)])

    def piece(index):
        block = lax.dynamic_slice(attn_in, (0, 0, index * chunk), (rows, 3, chunk))
        return block.transpose(1, 0, 2)

    sent = list(lax.optimization_barrier([piece(me ^ s) for s in range(PLANE)]))
    pieces = [sent[0]] + [swap(sent[s], s) for s in range(1, PLANE)]
    both_up = climb(weights, 1)
    both_down = climb(after(weights, rim), -1)
    product = (hyena_in[:, 0].astype(jnp.float32) * hyena_in[:, 2].astype(jnp.float32)).astype(
        jnp.bfloat16
    )
    hyena_act = fir(rim, product, hyena_in[:, 1], filters)
    hyena_act, *pieces = lax.optimization_barrier((hyena_act, *pieces))

    pairs = jnp.stack([p[1:] for p in pieces])
    queries = jnp.stack([p[0] for p in lax.optimization_barrier([pairs] + pieces)[1:]])
    lower_pairs = move(pairs, 1, 0, levels - 3)
    upper_queries = climb(queries, -1)
    hyena_one = swap(after(hyena_act, queries), 1)
    own = attend("causal", True, flags(me, 1), queries, pairs)
    top = levels - 2
    both_up = after(both_up, own[0])
    both_top = move(both_up, 1, top, top)
    hyena_rest, attn_rest = lax.optimization_barrier((both_up[0], both_up[1]))
    upper_queries, both_down, hyena_one = lax.optimization_barrier(
        (after(upper_queries, hyena_rest), both_down, hyena_one)
    )
    hyena_rest = move(after(hyena_rest, upper_queries), 1, 1, top - 1)
    hyena_down2 = climb(both_down[0], -1, 2)
    hyena_pair = jnp.stack([hyena_act, hyena_one])
    hyena_other = swap(hyena_pair, 2)
    carry = attend("full", False, flags(me, 1), upper_queries, pairs)
    lower_pairs, attn_down2 = lax.optimization_barrier((after(lower_pairs, carry[0]), both_down[1]))
    attn_down2 = climb(attn_down2, -1, 2)
    served = attend(
        "anti", True, flags(me, level > 0), upper_queries, lower_pairs, carry, jnp.bfloat16
    )
    served, both_top, hyena_down2 = lax.optimization_barrier((served, both_top, hyena_down2))
    hyena_rest, served = lax.optimization_barrier((hyena_rest, served))
    partial_up = climb(served, 1)
    attn_rest = move(after(attn_rest, served), 1, 1, top - 1)
    hyena_ups = [both_top[0] + after(hyena_rest, served)]
    hyena_downs = [hyena_down2]
    attn_ups, attn_downs = [], [attn_down2]
    for step in range(3, levels):
        hyena_ups.append(climb(hyena_ups[-1], 1, step))
        hyena_downs.append(climb(after(hyena_downs[-1], attn_down2), -1, step))
    attended = merge(flags(level > 0), *own, after(partial_up, hyena_ups[0], hyena_other))
    dep = [attended, hyena_ups[-1], hyena_downs[-1]]
    attn_ups.append(after(attn_rest, *dep))
    for step in range(3, levels):
        attn_ups.append(climb(attn_ups[-1], 1, step))
        attn_downs.append(climb(after(attn_downs[-1], hyena_downs[-1], attended), -1, step))
    hyena_parts = [(hyena_pair, 0), (hyena_pair, 1), (hyena_other, 0), (hyena_other, 1)]

    def blocks(layer, ups, downs, direct):
        found = [
            (weights, layer, 0, 0, levels - 1),
            (both_up, layer, -1, 1, levels - 1),
            (both_down, layer, 1, 0, levels - 2),
            (ups[0], 0, -2, 2, levels - 2 if direct else levels - 1),
        ]
        if direct:
            found.append((both_top, layer, -2, levels - 1, levels - 1))
        found += [(w, 0, -k, k, levels - 1) for k, w in enumerate(ups[1:], 3)]
        return found + [(w, 0, k, 0, levels - 1 - k) for k, w in enumerate(downs, 2)]

    def add_up(mine, others):
        gots = [
            lax.ppermute(others[shift - 1], "tp", [(i, (i + shift) % n_tp) for i in range(n_tp)])
            for shift in range(1, n_tp)
        ]
        pieces = []
        for s in range(PLANE):
            total = mine[s].astype(jnp.float32)
            for got in gots:
                total = total + got[s].astype(jnp.float32)
            pieces.append(total.astype(jnp.bfloat16))
        return pieces

    def exchange(pieces):
        return [pieces[0]] + [swap(pieces[s], s) for s in range(1, PLANE)]

    where = flags(level, group)
    attn_one, attn_two = swap(attended, 1), swap(attended, 2)
    hyena_parts[0] = (after(hyena_parts[0][0], attn_ups[0]), 0)
    hyena_blocks = blocks(0, hyena_ups, hyena_downs, False)
    hyena_terms = project(levels, n_tp, where, hyena_parts, hyena_blocks, CHEAP)
    attn_one, attn_two, attn_ups[0] = lax.optimization_barrier((attn_one, attn_two, attn_ups[0]))
    hyena_pieces = add_up(*hyena_terms)
    half = PLANE // 2
    attn_three = [swap(attn_one[:half], 2), swap(attn_two[half:], 1)]
    hyena_pieces = [after(p, *attn_three) for p in hyena_pieces]
    attn_three = jnp.concatenate(attn_three, 0)
    hyena_pieces = exchange(hyena_pieces)
    attn_parts = [attended, attn_one, attn_two, attn_three]
    attn_blocks = blocks(1, attn_ups, attn_downs, True)
    attn_terms = project(levels, n_tp, where, attn_parts, attn_blocks, CHEAP)
    hyena_pieces = [after(p, *attn_terms) for p in hyena_pieces]
    attn_pieces = add_up(*attn_terms)
    attn_pieces = exchange(attn_pieces)
    return assemble(flags(me), hyena_pieces), assemble(flags(me), attn_pieces)


def solution(mesh):
    in_specs = (
        P("ctx", None, "tp"),
        P(None, "tp"),
        P("ctx", None, "tp"),
        P("tp", "ctx"),
        P("tp", "ctx"),
    )
    out_specs = (P("ctx", "tp"), P("ctx", "tp"))
    return jax.shard_map(
        per_device, mesh=mesh, in_specs=in_specs, out_specs=out_specs, check_vma=False
    )
```

```python
import functools
import math

import jax
import jax.numpy as jnp
import ml_dtypes
import numpy as np
from jax import lax
from jax.experimental import pallas as pl
from jax.experimental.pallas import tpu as pltpu
from jax.sharding import PartitionSpec as P

HEAD_DIM = 128
WINDOW = 2048
PLANE = 4
MASKED = -1e30
LEVEL_ROWS = 16
VMEM = 56 * 1024 * 1024
CHEAP = pl.CostEstimate(flops=1, bytes_accessed=1, transcendentals=0)
MODEST = pl.CostEstimate(flops=2 * 10**9, bytes_accessed=1, transcendentals=0)
LARGE = pl.CostEstimate(flops=10**10, bytes_accessed=1, transcendentals=0)
ATTEND_COST = {"causal": LARGE, "full": CHEAP, "anti": LARGE}


def split_bf16(array):
    high = array.astype(jnp.bfloat16)
    return high, (array - high.astype(jnp.float32)).astype(jnp.bfloat16)


def mm(a, b):
    return jnp.dot(a, b, preferred_element_type=jnp.float32)


def dft_matrices(taps):
    size = 2 * taps
    n = np.arange(size)
    k = np.arange(taps)
    angle = 2 * np.pi * ((k[:, None] * n[None, :]) % size) / size
    cosine, sine = np.cos(angle), np.sin(angle)
    forward = np.concatenate([cosine, -sine], 0)
    forward[taps] = (-1.0) ** n
    weight = np.full(taps, 2.0 / size)
    weight[0] = 1.0 / size
    inverse = np.concatenate([cosine * weight[:, None], -sine * weight[:, None]], 0)
    inverse[taps] = (-1.0) ** n / size
    inverse = inverse.T[taps:]

    def halves(array):
        array = array.astype(np.float32)
        high = array.astype(ml_dtypes.bfloat16)
        return high, (array - high.astype(np.float32)).astype(ml_dtypes.bfloat16)

    return [jnp.asarray(m) for m in halves(forward) + halves(inverse)]


def fir_kernel(rim, product, gate, filters, f_hi, f_lo, g_hi, g_lo, out):
    taps = filters.shape[0]
    rows = product.shape[0]
    h_hi, h_lo = split_bf16(filters[...])
    spectrum = (
        mm(f_hi[:, :taps], h_hi) + mm(f_hi[:, :taps], h_lo) + mm(f_lo[:, :taps], h_hi)
    )
    first = lax.broadcasted_iota(jnp.int32, (taps, spectrum.shape[1]), 0) == 0
    h_re, h_im = spectrum[:taps], spectrum[taps:]
    h_re2 = jnp.where(first, h_im, h_re)
    h_im = jnp.where(first, 0.0, h_im)
    for start in range(0, rows, taps):
        before = rim[...] if start == 0 else product[start - taps : start]
        x = jnp.concatenate([before, product[start : start + taps]], 0)
        xs = mm(f_hi[...], x) + mm(f_lo[...], x)
        x_re, x_im = xs[:taps], xs[taps:]
        y = jnp.concatenate([x_re * h_re - x_im * h_im, x_re * h_im + x_im * h_re2], 0)
        y_hi, y_lo = split_bf16(y)
        filtered = mm(g_hi[...], y_hi) + mm(g_hi[...], y_lo) + mm(g_lo[...], y_hi)
        span = slice(start, start + taps)
        out[span] = (gate[span].astype(jnp.float32) * filtered).astype(out.dtype)


@jax.named_scope('fir')
def fir(rim, product, gate, filters):
    taps, width = filters.shape
    rows = product.shape[0]
    tile = min(512, width)
    mats = dft_matrices(taps)
    column = lambda n: pl.BlockSpec((n, tile), lambda i: (0, i))
    return pl.pallas_call(
        fir_kernel,
        grid=(width // tile,),
        in_specs=[column(taps), column(rows), column(rows), column(taps)]
        + [pl.BlockSpec(m.shape, lambda i: (0, 0)) for m in mats],
        out_specs=column(rows),
        out_shape=jax.ShapeDtypeStruct((rows, width), jnp.bfloat16),
        compiler_params=pltpu.CompilerParams(vmem_limit_bytes=VMEM),
        cost_estimate=CHEAP,
    )(rim, product, gate, filters, *mats)


def pack_level(level):
    pieces, rest = [], level
    for _ in range(3):
        term = rest.astype(jnp.bfloat16).astype(jnp.float32)
        pieces += [term[:, c : c + HEAD_DIM] for c in range(0, level.shape[1], HEAD_DIM)]
        rest = rest - term
    pieces += [jnp.zeros((LEVEL_ROWS - len(pieces), HEAD_DIM), jnp.float32)]
    return jnp.concatenate(pieces, 0).astype(jnp.bfloat16)


def unpack_level(block, rows):
    block = block.astype(jnp.float32)
    count = rows // HEAD_DIM
    total = block[0:count] + block[count : 2 * count] + block[2 * count : 3 * count]
    return jnp.concatenate([total[c : c + 1] for c in range(count)], 1)


def attend_kernel(kind, first, last, info, q_ref, k_ref, v_ref, *refs):
    refs = list(refs)
    if not first:
        acc_in, stat_in = refs.pop(0), refs.pop(0)
    packed = len(refs) == 1
    out, stat_out = refs[0], refs[-1]
    plane, rows = k_ref.shape[0], k_ref.shape[2]
    me = info[0]
    factor = math.log2(math.e) / math.sqrt(HEAD_DIM)
    half = HEAD_DIM // 2

    def write(i, top, total, acc):
        if last:
            out[me ^ i, :rows] = (acc * (1.0 / total)).astype(out.dtype)
            level = jnp.broadcast_to(top + jnp.log2(total), (rows, HEAD_DIM)).T[0:1]
            if packed:
                out[me ^ i, rows:] = pack_level(level)
            else:
                stat_out[0, me ^ i] = jnp.broadcast_to(level, (8, rows))
        else:
            out[me ^ i] = acc
            lane = lax.broadcasted_iota(jnp.int32, (rows, HEAD_DIM), 1)
            stat_out[me ^ i] = jnp.where(lane < half, top, total)

    def previous(i):
        stat = stat_in[me ^ i]
        return stat[:, 0:1], stat[:, half : half + 1], acc_in[me ^ i]

    def attend(i):
        blocks = range(plane)
        if kind != "full":
            blocks = range(i + 1) if kind == "causal" else range(i, plane)
        q = q_ref[me ^ i]
        scores = []
        for j in blocks:
            s = lax.dot_general(
                q, k_ref[me ^ j, 0], (((1,), (1,)), ((), ())), preferred_element_type=jnp.float32
            ) * factor
            if j == i and kind != "full":
                row = lax.broadcasted_iota(jnp.int32, s.shape, 0)
                col = lax.broadcasted_iota(jnp.int32, s.shape, 1)
                s = jnp.where(col <= row if kind == "causal" else col > row, s, MASKED)
            scores.append(s)
        top = functools.reduce(jnp.maximum, scores).max(axis=1, keepdims=True)
        if not first:
            old_top, old_total, old_acc = previous(i)
            top = jnp.maximum(top, old_top)
        acc, sums = None, None
        for j, s in zip(blocks, scores):
            w = jnp.exp2(s - top)
            sums = w if sums is None else sums + w
            term = mm(w.astype(jnp.bfloat16), v_ref[me ^ j, 0])
            acc = term if acc is None else acc + term
        total = sums.sum(axis=1, keepdims=True)
        if not first:
            shrink = jnp.exp2(old_top - top)
            total = total + shrink * old_total
            acc = acc + shrink * old_acc
        write(i, top, total, acc)

    def run():
        for i in range(plane):
            attend(i)

    if first:
        run()
    else:

        @pl.when(info[1] > 0)
        def _():
            run()

        @pl.when(info[1] == 0)
        def _():
            for i in range(plane):
                write(i, *previous(i))


def attend(kind, last, info, queries, pairs, carry=(), dtype=jnp.float32):
    plane, rows, width = queries.shape
    heads = width // HEAD_DIM
    mine = pl.BlockSpec((plane, rows, HEAD_DIM), lambda h, info: (0, 0, h))
    keys = pl.BlockSpec((plane, 1, rows, HEAD_DIM), lambda h, info: (0, 0, 0, h))
    values = pl.BlockSpec((plane, 1, rows, HEAD_DIM), lambda h, info: (0, 1, 0, h))
    state = jax.ShapeDtypeStruct(queries.shape, jnp.float32)
    if last and dtype == jnp.bfloat16:
        tall = (plane, rows + LEVEL_ROWS)
        out_specs = pl.BlockSpec(tall + (HEAD_DIM,), lambda h, info: (0, 0, h))
        out_shape = jax.ShapeDtypeStruct(tall + (width,), dtype)
    elif last:
        out_specs = (mine, pl.BlockSpec((1, plane, 8, rows), lambda h, info: (h, 0, 0, 0)))
        out_shape = (
            jax.ShapeDtypeStruct(queries.shape, dtype),
            jax.ShapeDtypeStruct((heads, plane, 8, rows), jnp.float32),
        )
    else:
        out_specs, out_shape = (mine, mine), (state, state)
    return pl.pallas_call(
        functools.partial(attend_kernel, kind, not carry, last),
        grid_spec=pltpu.PrefetchScalarGridSpec(
            num_scalar_prefetch=1,
            grid=(heads,),
            in_specs=[mine, keys, values] + [mine] * len(carry),
            out_specs=out_specs,
        ),
        out_shape=out_shape,
        compiler_params=pltpu.CompilerParams(vmem_limit_bytes=VMEM),
        cost_estimate=ATTEND_COST[kind],
    )(info, queries, pairs, pairs, *carry)


def merge_kernel(info, one_ref, level_one, two_ref, out):
    rows = one_ref.shape[1]
    for h in range(one_ref.shape[2] // HEAD_DIM):
        span = slice(h * HEAD_DIM, (h + 1) * HEAD_DIM)
        one, two = level_one[h, 0, 0:1], unpack_level(two_ref[0, rows:, span], rows)
        two = jnp.where(info[0] > 0, two, MASKED)
        top = jnp.maximum(one, two)
        one, two = jnp.exp2(one - top), jnp.exp2(two - top)
        share = jnp.broadcast_to(two * (1.0 / (one + two)), (HEAD_DIM, rows)).T
        first, second = one_ref[0, :, span], two_ref[0, :rows, span].astype(jnp.float32)
        out[0, :, span] = (first + share * (second - first)).astype(out.dtype)


@jax.named_scope('merge')
def merge(info, one, level_one, two):
    plane, rows, width = one.shape
    block = pl.BlockSpec((1, rows, width), lambda i, info: (i, 0, 0))
    level = pl.BlockSpec((level_one.shape[0], 1, 8, rows), lambda i, info: (0, i, 0, 0))
    return pl.pallas_call(
        merge_kernel,
        grid_spec=pltpu.PrefetchScalarGridSpec(
            num_scalar_prefetch=1,
            grid=(plane,),
            in_specs=[
                block,
                level,
                pl.BlockSpec((1,) + two.shape[1:], lambda i, info: (i, 0, 0)),
            ],
            out_specs=block,
        ),
        out_shape=jax.ShapeDtypeStruct(one.shape, jnp.bfloat16),
        compiler_params=pltpu.CompilerParams(vmem_limit_bytes=VMEM),
        cost_estimate=MODEST,
    )(info, one, level_one, two)


def project_kernel(levels, n_tp, part_index, weight_index, info, *refs):
    splits = len(part_index)
    parts, weights = refs[:splits], refs[splits:-8]
    mine, others, a, w, y, sem_a, sem_w, sem_y = refs[-8:]
    level, group = info[0], info[1]
    plane, rows, columns = y.shape[1:]
    depth = a.shape[1] // plane
    share = levels // n_tp

    loads = []
    for part, (s, index, base) in zip(parts, part_index):
        if index is not None:
            copy = pltpu.make_async_copy(part.at[index], a.at[pl.ds(s * rows, rows)], sem_a.at[s])
            loads.append(copy)
            continue
        for r in range(plane):
            if not base <= r ^ s < base + part.shape[0]:
                continue
            loads.append(
                pltpu.make_async_copy(
                    part.at[(r ^ s) - base],
                    a.at[pl.ds(r * rows, rows), pl.ds(s * depth, depth)],
                    sem_a.at[s * plane + r],
                )
            )
    for copy in loads:
        copy.start()
    for weight, (index, offset, first, last) in zip(weights, weight_index):
        target = level + offset

        @pl.when((level >= first) & (level <= last))
        def _(weight=weight, index=index, target=target):
            pltpu.make_async_copy(weight.at[index], w.at[target], sem_w.at[target]).start()

    def store(t, act):
        ahead = (t // share + n_tp - group) % n_tp

        @pl.when(ahead == 0)
        def _():
            act(pltpu.make_async_copy(y.at[t], mine.at[:, t % share], sem_y.at[t]))

        @pl.when(ahead > 0)
        def _():
            act(pltpu.make_async_copy(y.at[t], others.at[ahead - 1, :, t % share], sem_y.at[t]))

    for copy in loads:
        copy.wait()
    for t in range(levels):
        pltpu.make_async_copy(weights[0].at[0], w.at[t], sem_w.at[t]).wait()
        for r in range(plane):
            y[t, r] = mm(a[r * rows : (r + 1) * rows], w[t]).astype(y.dtype)
        store(t, lambda copy: copy.start())
    for t in range(levels):
        store(t, lambda copy: copy.wait())


@jax.named_scope('project')
def project(levels, n_tp, info, parts, weights, cost=CHEAP):
    pieces = []
    for s, part in enumerate(parts):
        if isinstance(part, list):
            pieces += [(p, s, None, i * p.shape[0]) for i, p in enumerate(part)]
        elif isinstance(part, tuple):
            pieces.append((part[0], s, part[1], 0))
        else:
            pieces.append((part, s, None, 0))
    parts = pieces
    weights = [(w[0][None], 0, *w[2:]) if w[0].ndim == 2 else w for w in weights]
    width, columns = weights[0][0].shape[1:]
    rows = parts[0][0].shape[1]
    block = (PLANE, levels // n_tp, rows, columns)
    anywhere = pl.BlockSpec(memory_space=pl.ANY)
    return pl.pallas_call(
        functools.partial(
            project_kernel, levels, n_tp, [p[1:] for p in parts], [w[1:] for w in weights]
        ),
        grid_spec=pltpu.PrefetchScalarGridSpec(
            num_scalar_prefetch=1,
            grid=(1,),
            in_specs=[anywhere] * (len(parts) + len(weights)),
            out_specs=(anywhere, anywhere),
            scratch_shapes=[
                pltpu.VMEM((PLANE * rows, width), jnp.bfloat16),
                pltpu.VMEM((levels, width, columns), jnp.bfloat16),
                pltpu.VMEM((levels, PLANE, rows, columns), jnp.bfloat16),
                pltpu.SemaphoreType.DMA((PLANE * PLANE,)),
                pltpu.SemaphoreType.DMA((levels,)),
                pltpu.SemaphoreType.DMA((levels,)),
            ],
        ),
        out_shape=(
            jax.ShapeDtypeStruct(block, jnp.bfloat16),
            jax.ShapeDtypeStruct((n_tp - 1,) + block, jnp.bfloat16),
        ),
        compiler_params=pltpu.CompilerParams(vmem_limit_bytes=VMEM),
        cost_estimate=cost,
    )(info, *[p[0] for p in parts], *[w[0] for w in weights])


def assemble_kernel(info, *refs):
    pieces, out = refs[:-1], refs[-1]
    share, rows, columns = pieces[0].shape
    for s, piece in enumerate(pieces):
        for t in range(share):
            start = pl.multiple_of((t * PLANE + (info[0] ^ s)) * columns, columns)
            out[:, pl.ds(start, columns)] = piece[t]


@jax.named_scope('assemble')
def assemble(info, pieces):
    share, rows, columns = pieces[0].shape
    if columns % 128:
        natural = [
            lax.select_n(info[0], *[pieces[t ^ j] for t in range(PLANE)]) for j in range(PLANE)
        ]
        return jnp.stack(natural, 1).transpose(2, 0, 1, 3).reshape(rows, -1)
    return pl.pallas_call(
        assemble_kernel,
        grid_spec=pltpu.PrefetchScalarGridSpec(
            num_scalar_prefetch=1,
            grid=(1,),
            in_specs=[pl.BlockSpec(p.shape, lambda i, info: (0, 0, 0)) for p in pieces],
            out_specs=pl.BlockSpec((rows, share * PLANE * columns), lambda i, info: (0, 0)),
        ),
        out_shape=jax.ShapeDtypeStruct((rows, share * PLANE * columns), jnp.bfloat16),
        compiler_params=pltpu.CompilerParams(vmem_limit_bytes=VMEM),
        cost_estimate=CHEAP,
    )(info, *pieces)


def per_device(hyena_in, filters, attn_in, out_weight, attn_weight):
    rows, _, width = hyena_in.shape
    taps = filters.shape[0]
    n_ctx, n_tp = lax.axis_size("ctx"), lax.axis_size("tp")
    levels = n_ctx // PLANE
    device_index = lax.axis_index("ctx")
    group = lax.axis_index("tp")
    me, level = device_index % PLANE, device_index // PLANE
    chunk = width // PLANE
    assert WINDOW == 2 * PLANE * rows and levels > 2 and levels % n_tp == 0

    def flags(*values):
        return jnp.stack([jnp.asarray(v).astype(jnp.int32) for v in values])

    def after(value, *others):
        return lax.optimization_barrier((value, *others))[0]

    def swap(block, relative):
        return lax.ppermute(block, "ctx", [(i, i ^ relative) for i in range(n_ctx)])

    def move(block, direction, first, last):
        sources = range(first * PLANE, (last + 1) * PLANE)
        return lax.ppermute(block, "ctx", [(i, i + direction * PLANE) for i in sources])

    def climb(block, direction, step=1):
        if direction > 0:
            return move(block, 1, step - 1, levels - 2)
        return move(block, -1, 1, levels - step)

    last_rows = hyena_in[rows - taps :]
    rim = (last_rows[:, 0].astype(jnp.float32) * last_rows[:, 2].astype(jnp.float32)).astype(
        jnp.bfloat16
    )
    attn_rows = attn_weight.reshape(PLANE, chunk, -1)
    attn_weight = jnp.concatenate(
        [lax.dynamic_index_in_dim(attn_rows, me ^ s, 0, False) for s in range(PLANE)], 0
    )
    weights = after(jnp.stack([out_weight, attn_weight]), rim)
    attn_in = after(attn_in, weights)
    rim = lax.ppermute(rim, "ctx", [(i, i + 1) for i in range(n_ctx - 1)])

    def piece(index):
        block = lax.dynamic_slice(attn_in, (0, 0, index * chunk), (rows, 3, chunk))
        return block.transpose(1, 0, 2)

    sent = list(lax.optimization_barrier([piece(me ^ s) for s in range(PLANE)]))
    pieces = [sent[0]] + [swap(sent[s], s) for s in range(1, PLANE)]
    both_up = climb(weights, 1)
    both_down = climb(after(weights, rim), -1)
    product = (hyena_in[:, 0].astype(jnp.float32) * hyena_in[:, 2].astype(jnp.float32)).astype(
        jnp.bfloat16
    )
    hyena_act = fir(rim, product, hyena_in[:, 1], filters)
    hyena_act, *pieces = lax.optimization_barrier((hyena_act, *pieces))

    pairs = jnp.stack([p[1:] for p in pieces])
    queries = jnp.stack([p[0] for p in lax.optimization_barrier([pairs] + pieces)[1:]])
    lower_pairs = move(pairs, 1, 0, levels - 3)
    upper_queries = climb(queries, -1)
    hyena_one = swap(after(hyena_act, queries), 1)
    own = attend("causal", True, flags(me, 1), queries, pairs)
    top = levels - 2
    both_up = after(both_up, own[0])
    both_top = move(both_up, 1, top, top)
    hyena_rest, attn_rest = lax.optimization_barrier((both_up[0], both_up[1]))
    upper_queries, both_down, hyena_one = lax.optimization_barrier(
        (after(upper_queries, hyena_rest), both_down, hyena_one)
    )
    hyena_rest = move(after(hyena_rest, upper_queries), 1, 1, top - 1)
    hyena_down2 = climb(both_down[0], -1, 2)
    hyena_pair = jnp.stack([hyena_act, hyena_one])
    hyena_other = swap(hyena_pair, 2)
    carry = attend("full", False, flags(me, 1), upper_queries, pairs)
    lower_pairs, attn_down2 = lax.optimization_barrier((after(lower_pairs, carry[0]), both_down[1]))
    attn_down2 = climb(attn_down2, -1, 2)
    served = attend(
        "anti", True, flags(me, level > 0), upper_queries, lower_pairs, carry, jnp.bfloat16
    )
    served, both_top, hyena_down2 = lax.optimization_barrier((served, both_top, hyena_down2))
    hyena_rest, served = lax.optimization_barrier((hyena_rest, served))
    partial_up = climb(served, 1)
    attn_rest = move(after(attn_rest, served), 1, 1, top - 1)
    hyena_ups = [both_top[0] + after(hyena_rest, served)]
    hyena_downs = [hyena_down2]
    attn_ups, attn_downs = [], [attn_down2]
    for step in range(3, levels):
        hyena_ups.append(climb(hyena_ups[-1], 1, step))
        hyena_downs.append(climb(after(hyena_downs[-1], attn_down2), -1, step))
    attended = merge(flags(level > 0), *own, after(partial_up, hyena_ups[0], hyena_other))
    dep = [attended, hyena_ups[-1], hyena_downs[-1]]
    attn_ups.append(after(attn_rest, *dep))
    for step in range(3, levels):
        attn_ups.append(climb(attn_ups[-1], 1, step))
        attn_downs.append(climb(after(attn_downs[-1], hyena_downs[-1], attended), -1, step))
    hyena_parts = [(hyena_pair, 0), (hyena_pair, 1), (hyena_other, 0), (hyena_other, 1)]

    def blocks(layer, ups, downs, direct):
        found = [
            (weights, layer, 0, 0, levels - 1),
            (both_up, layer, -1, 1, levels - 1),
            (both_down, layer, 1, 0, levels - 2),
            (ups[0], 0, -2, 2, levels - 2 if direct else levels - 1),
        ]
        if direct:
            found.append((both_top, layer, -2, levels - 1, levels - 1))
        found += [(w, 0, -k, k, levels - 1) for k, w in enumerate(ups[1:], 3)]
        return found + [(w, 0, k, 0, levels - 1 - k) for k, w in enumerate(downs, 2)]

    def add_up(mine, others):
        gots = [
            lax.ppermute(others[shift - 1], "tp", [(i, (i + shift) % n_tp) for i in range(n_tp)])
            for shift in range(1, n_tp)
        ]
        pieces = []
        for s in range(PLANE):
            total = mine[s].astype(jnp.float32)
            for got in gots:
                total = total + got[s].astype(jnp.float32)
            pieces.append(total.astype(jnp.bfloat16))
        return pieces

    def exchange(pieces):
        return [pieces[0]] + [swap(pieces[s], s) for s in range(1, PLANE)]

    where = flags(level, group)
    attn_one, attn_two = swap(attended, 1), swap(attended, 2)
    hyena_parts[0] = (after(hyena_parts[0][0], attn_ups[0]), 0)
    hyena_blocks = blocks(0, hyena_ups, hyena_downs, False)
    hyena_terms = project(levels, n_tp, where, hyena_parts, hyena_blocks, CHEAP)
    attn_one, attn_two, attn_ups[0] = lax.optimization_barrier((attn_one, attn_two, attn_ups[0]))
    hyena_pieces = add_up(*hyena_terms)
    half = PLANE // 2
    attn_three = [swap(attn_one[:half], 2), swap(attn_two[half:], 1)]
    hyena_pieces = [after(p, *attn_three) for p in hyena_pieces]
    hyena_pieces = exchange(hyena_pieces)
    attn_parts = [attended, attn_one, attn_two, attn_three]
    attn_blocks = blocks(1, attn_ups, attn_downs, True)
    attn_terms = project(levels, n_tp, where, attn_parts, attn_blocks, CHEAP)
    hyena_pieces = [after(p, *attn_terms) for p in hyena_pieces]
    attn_pieces = add_up(*attn_terms)
    attn_pieces = exchange(attn_pieces)
    return assemble(flags(me), hyena_pieces), assemble(flags(me), attn_pieces)


def solution(mesh):
    in_specs = (
        P("ctx", None, "tp"),
        P(None, "tp"),
        P("ctx", None, "tp"),
        P("tp", "ctx"),
        P("tp", "ctx"),
    )
    out_specs = (P("ctx", "tp"), P("ctx", "tp"))
    return jax.shard_map(
        per_device, mesh=mesh, in_specs=in_specs, out_specs=out_specs, check_vma=False
    )
```
